512 devices in a mesh: blk: 16 (over z_lo, x, core), dp: 32 (over z_hi, y).
Axes of the slice: x: 4, y: 8, z: 8 (z_hi: 4, z_lo: 2; z = z_hi * 2 + z_lo), core: 2. Of those that a mesh axis runs over, the one named last changes fastest.
Arguments:
- queries: bfloat16 [65536, 1024], P(('blk', 'dp')), may hold values from -0.5 to 0.5, as said below
- passages: bfloat16 [65536, 1024], P(('blk', 'dp')), may hold values from -0.5 to 0.5, as said below
- positive: int32 [65536], P(('blk', 'dp')), may hold values from 0 to 2047, as said below
- hard_ids: int32 [65536, 4], P(('blk', 'dp')), may hold values from 0 to 4095, as said below
- hard_count: int32 [65536], P(('blk', 'dp')), may hold values from 1 to 4
Outputs:
- query_grads: bfloat16 [65536, 1024], P(('blk', 'dp'))
- passage_grads: bfloat16 [65536, 1024], P(('blk', 'dp'))
The draws below stay inside these ranges and needn't reach their ends.
Inputs may be any that keep to these rules, and one draw needn't show every extreme that they name: `queries`: encoder outputs. `passages`: encoder outputs. `positive`: index into the query's in-batch group. `hard_ids`: entry e names row e % 128 of the device with the query's blk index and dp index e // 128; among the rows of one device, at most 32 entries name one dp index, and exactly 32 entries name some dp index.
All inputs are finite; a program needn't handle non-finite values.
Results may differ from the reference program's by a relative error of at most 0.0079.
Values may be sent and summed in bfloat16 or wider, within the bound.
No kernel may reach another device: no remote copies, remote signals or barrier semaphores. Data moves between devices by JAX's collectives and lax.ppermute only.
A program may use at most 64 MiB of HBM per device.

```python
import jax
import jax.numpy as jnp
from jax import lax

D = 1024
ROWS = 128
HMAX = 4
GROUP = 2048
QUERIES = 65536
N_BLK = 16
N_DP = 32


def mixed_rows(key, count):
    first = jax.random.fold_in(key, 0)
    gauss = jnp.clip(jax.random.normal(first, (count, D), jnp.float32), -6.0, 6.0)
    return gauss * 0.03125


def topic_centres(key):
    key = jax.random.fold_in(key, 404)
    key_centre, key_perm = jax.random.split(key)
    centres = mixed_rows(key_centre, N_DP * ROWS)
    devices = QUERIES // ROWS
    orders = jax.vmap(lambda k: jax.random.permutation(k, ROWS))(jax.random.split(key_perm, devices))
    dp_index = jnp.arange(devices, dtype=jnp.int32) % N_DP
    topic = (dp_index[:, None] * ROWS + orders.astype(jnp.int32)).reshape(QUERIES)
    return centres[topic]


def passage_parts(key):
    noise = mixed_rows(jax.random.fold_in(key, 101), QUERIES)
    centre = topic_centres(key)
    return (centre, noise)


def hard_table(key):
    key = jax.random.fold_in(key, 202)
    devices = QUERIES // ROWS
    slots = ROWS * HMAX
    limit = 2 * slots // N_DP
    key_busy, key_offset, key_order, key_row = jax.random.split(key, 4)
    busy = jax.random.randint(key_busy, (devices, 1), 0, N_DP)
    offset = jax.random.randint(key_offset, (devices, 1), 0, N_DP - 1)
    place = jnp.arange(slots, dtype=jnp.int32)[None, :]
    rest = (place - limit) % (N_DP - 1)
    other = (busy + 1 + (rest + offset) % (N_DP - 1)) % N_DP
    owner = jnp.where(place < limit, busy, other)
    order = jax.vmap(lambda k: jax.random.permutation(k, slots))(jax.random.split(key_order, devices))
    owner = jnp.take_along_axis(owner, order, axis=1)
    row = jax.random.randint(key_row, (devices, slots), 0, ROWS)
    return (owner * ROWS + row).reshape(QUERIES, HMAX).astype(jnp.int32)


def positive_table(key):
    return jax.random.randint(jax.random.fold_in(key, 303), (QUERIES,), 0, GROUP).astype(jnp.int32)


def draw_passages(key, part):
    centre, noise = passage_parts(key)
    return (0.6 * centre + 0.8 * noise).astype(jnp.bfloat16)


def draw_positive(key, part):
    return positive_table(key)


def draw_hard_ids(key, part):
    return hard_table(key)


def draw_queries(key, part):
    own_key = jax.random.fold_in(key, 11)
    centre, noise = passage_parts(key)
    passages = 0.6 * centre + 0.8 * noise
    hard = hard_table(key)
    positive = positive_table(key)
    own_noise = mixed_rows(own_key, QUERIES)
    device = jnp.arange(QUERIES, dtype=jnp.int32) // ROWS
    blk_index = device // N_DP
    dp_index = device % N_DP
    pos_global = (positive // ROWS * N_DP + dp_index) * ROWS + positive % ROWS
    mixed = 0.32 * centre[pos_global] + 0.8 * own_noise + 0.06 * noise[pos_global]
    for entry in range(HMAX):
        hard_global = (blk_index * N_DP + hard[:, entry] // ROWS) * ROWS + hard[:, entry] % ROWS
        mixed = mixed + 0.21 * passages[hard_global]
    return mixed.astype(jnp.bfloat16)


def touch_ends(drawn, key, smallest, largest):
    longest = drawn.shape.index(max(drawn.shape))
    spots = []
    for shift in (0, 1):
        where = [jax.random.randint(jax.random.fold_in(key, axis), (), 0, length) for axis, length in enumerate(drawn.shape)]
        where[longest] = (where[longest] + shift) % drawn.shape[longest]
        spots.append(tuple(where))
    return drawn.at[spots[0]].set(smallest).at[spots[1]].set(largest)


def setup_inputs(seed: int = 0) -> dict:
    key_list = jax.random.split(jax.random.key(seed), 6)
    return {
        "queries": draw_queries(jax.random.fold_in(key_list[5], 71), 0),
        "passages": draw_passages(jax.random.fold_in(key_list[5], 71), 0),
        "positive": draw_positive(jax.random.fold_in(key_list[5], 71), 0),
        "hard_ids": draw_hard_ids(jax.random.fold_in(key_list[5], 71), 0),
        "hard_count": touch_ends(jax.random.randint(key_list[4], (QUERIES,), 1, HMAX + 1), jax.random.fold_in(key_list[4], 1), 1, HMAX).astype(jnp.int32),
    }


EPS = 1e-06
TAU = 0.02

def unit_rows(x):
    xf = x.astype(jnp.float32)
    scale = lax.rsqrt(lax.optimization_barrier(jnp.sum(xf * xf, axis=1, keepdims=True)) + EPS)
    return (xf * scale, scale)

def tangent(unit, scale, direction):
    along = lax.optimization_barrier(jnp.sum(unit * direction, axis=1, keepdims=True))
    return (scale * (direction - unit * along)).astype(jnp.bfloat16)

def reference(queries, passages, positive, hard_ids, hard_count):
    q_unit, q_scale = unit_rows(queries)
    p_unit, p_scale = unit_rows(passages)
    q_half = q_unit.astype(jnp.bfloat16)
    p_half = p_unit.astype(jnp.bfloat16)
    q_blocks = jnp.swapaxes(q_half.reshape(N_BLK, N_DP, ROWS, D), 0, 1)
    p_blocks = jnp.swapaxes(p_half.reshape(N_BLK, N_DP, ROWS, D), 0, 1)
    pos_blocks = jnp.swapaxes(positive.reshape(N_BLK, N_DP, ROWS), 0, 1)
    hid_blocks = jnp.swapaxes(hard_ids.reshape(N_BLK, N_DP, ROWS, HMAX), 0, 1)
    cnt_blocks = jnp.swapaxes(hard_count.reshape(N_BLK, N_DP, ROWS), 0, 1)
    columns = p_half.reshape(N_BLK, N_DP * ROWS, D)

    def one_group(items):
        q_group, p_group, pos_group, hid_group, cnt_group = items
        group = p_group.reshape(GROUP, D)
        asking = q_group.reshape(GROUP, D)
        scores = jnp.dot(asking, group.T, preferred_element_type=jnp.float32) / TAU
        hard_rows = jax.vmap(lambda col, ids: col[ids])(columns, hid_group).reshape(GROUP, HMAX, D)
        hard_scores = jnp.einsum('rd,rkd->rk', asking.astype(jnp.float32), hard_rows.astype(jnp.float32), precision=lax.Precision.HIGHEST) / TAU
        mask = jnp.arange(HMAX, dtype=jnp.int32)[None, :] < cnt_group.reshape(GROUP)[:, None]
        exp_scores = jnp.exp(scores)
        exp_hard = jnp.where(mask, jnp.exp(hard_scores), jnp.float32(0.0))
        total = lax.optimization_barrier(jnp.sum(exp_scores, axis=1)) + lax.optimization_barrier(jnp.sum(exp_hard, axis=1))
        target = (pos_group.reshape(GROUP)[:, None] == jnp.arange(GROUP, dtype=jnp.int32)[None, :]).astype(jnp.float32)
        grad_block = (exp_scores / total[:, None] - target).astype(jnp.bfloat16)
        hard_weights = (exp_hard / total[:, None]).astype(jnp.bfloat16)
        q_dir = (jnp.dot(grad_block, group, preferred_element_type=jnp.float32) + jnp.einsum('rk,rkd->rd', hard_weights.astype(jnp.float32), hard_rows.astype(jnp.float32), precision=lax.Precision.HIGHEST)) / TAU
        p_group_dir = jnp.dot(grad_block.T, asking, preferred_element_type=jnp.float32) / TAU
        hard_grads = (hard_weights.astype(jnp.float32)[:, :, None] * asking.astype(jnp.float32)[:, None, :] / TAU).astype(jnp.bfloat16)
        return (q_dir, p_group_dir, hard_grads.reshape(N_BLK, ROWS * HMAX, D))
    q_dir, p_group_dir, hard_grads = lax.map(one_group, (q_blocks, p_blocks, pos_blocks, hid_blocks, cnt_blocks))
    q_dir = jnp.swapaxes(q_dir.reshape(N_DP, N_BLK, ROWS, D), 0, 1).reshape(QUERIES, D)
    p_group_dir = jnp.swapaxes(p_group_dir.reshape(N_DP, N_BLK, ROWS, D), 0, 1).reshape(QUERIES, D)
    hard_by_blk = jnp.swapaxes(hard_grads, 0, 1)
    ids_by_blk = hard_ids.reshape(N_BLK, N_DP * ROWS * HMAX)

    def one_column(items):
        grads, ids = items
        return jax.ops.segment_sum(grads.reshape(N_DP * ROWS * HMAX, D).astype(jnp.float32), ids, num_segments=N_DP * ROWS)
    hard_dir = lax.map(one_column, (hard_by_blk, ids_by_blk)).reshape(QUERIES, D)
    p_dir = p_group_dir + hard_dir
    return (tangent(q_unit, q_scale, q_dir), tangent(p_unit, p_scale, p_dir))
```

```python
import jax
import jax.numpy as jnp
from jax import lax
from jax.sharding import PartitionSpec as P

EPS = 1e-06
TAU = 0.02


def unit_rows(x):
    xf = x.astype(jnp.float32)
    scale = lax.rsqrt(jnp.sum(xf * xf, axis=1, keepdims=True) + EPS)
    return (xf * scale, scale)


def tangent(unit, scale, direction):
    along = jnp.sum(unit * direction, axis=1, keepdims=True)
    return (scale * (direction - unit * along)).astype(jnp.bfloat16)


def dot(a, b, ca, cb):
    return lax.dot_general(a, b, (((ca,), (cb,)), ((), ())), preferred_element_type=jnp.float32)


def local(queries, passages, positive, hard_ids, hard_count):
    rows, width = queries.shape
    hmax = hard_ids.shape[1]
    length = lax.axis_size("blk")
    peers = lax.axis_size("dp")
    me_blk = lax.axis_index("blk")
    me_dp = lax.axis_index("dp")
    limit = 2 * rows * hmax // peers
    slots = peers * limit
    entries = rows * hmax
    bf16 = jnp.bfloat16

    own_ids = hard_ids.T.reshape(entries)
    all_ids = lax.all_gather(own_ids, "dp", axis=0, tiled=False)

    q_unit, q_scale = unit_rows(queries)
    p_unit, p_scale = unit_rows(passages)
    q_half = q_unit.astype(bf16)
    p_half = p_unit.astype(bf16)
    p_group = lax.all_gather(p_half, "blk", axis=0, tiled=True)
    q_group = lax.all_gather(q_half, "blk", axis=0, tiled=True)

    owner = own_ids // rows
    number = jnp.arange(entries, dtype=jnp.int32)
    before = (owner[:, None] == owner[None, :]) & (number[None, :] < number[:, None])
    rank = jnp.sum(before.astype(jnp.int32), axis=1)
    place = (owner * limit + rank).reshape(hmax, rows)
    slot = jnp.arange(slots, dtype=jnp.int32)
    fills = jnp.any(place[:, :, None] == slot[None, None, :], axis=0)
    used = jnp.arange(hmax, dtype=jnp.int32)[:, None] < hard_count[None, :]
    used_place = jnp.where(used, place, -1)
    weighs = jnp.any(used_place[:, :, None] == slot[None, None, :], axis=0)

    sent_q = dot(fills.astype(bf16), q_half, 0, 0).astype(bf16)
    got_q = lax.all_to_all(
        sent_q.reshape(peers, limit, width), "dp", split_axis=0, concat_axis=0, tiled=True
    ).reshape(slots, width)

    mine = all_ids // rows == me_dp
    earlier = (number[:, None] < number[None, :]).astype(bf16)
    mine_rank = dot(mine.astype(bf16), earlier, 1, 0).astype(jnp.int32)
    mine_rank = jnp.where(mine, mine_rank, -1)
    in_slot = mine_rank[:, None, :] == jnp.arange(limit, dtype=jnp.int32)[None, :, None]
    asked = jnp.sum(jnp.where(in_slot, (all_ids % rows + 1)[:, None, :], 0), axis=2) - 1
    names = asked.reshape(1, slots) == jnp.arange(rows, dtype=jnp.int32)[:, None]

    sent_p = dot(names.astype(bf16), p_half, 0, 0).astype(bf16)
    sent_p, got_q = lax.optimization_barrier((sent_p, got_q))
    got_p = lax.all_to_all(
        sent_p.reshape(peers, limit, width), "dp", split_axis=0, concat_axis=0, tiled=True
    ).reshape(slots, width)

    cross = dot(p_half, got_q, 1, 1)
    made = jnp.sum(jnp.where(names, cross, 0.0), axis=0) / TAU
    all_made = lax.all_gather(made, "dp", axis=0, tiled=False)
    hard_scores = lax.dynamic_slice_in_dim(all_made, me_dp * limit, limit, 1).reshape(1, slots)
    exp_hard = jnp.where(weighs, jnp.exp(hard_scores), 0.0)

    scores = dot(q_half, p_group, 1, 1) / TAU
    exp_scores = jnp.exp(scores)
    total = jnp.sum(exp_scores, axis=1) + jnp.sum(exp_hard, axis=1)
    weights = (exp_hard / total[:, None]).astype(bf16)
    slot_weights = jnp.sum(weights.astype(jnp.float32), axis=0)
    all_weights = lax.all_gather(slot_weights, "dp", axis=0, tiled=False)
    got_weights = lax.dynamic_slice_in_dim(all_weights, me_dp * limit, limit, 1).reshape(1, slots)
    facts = lax.all_gather(
        jnp.stack([total, positive.astype(jnp.float32)]), "blk", axis=0, tiled=False
    )
    all_total = facts[:, 0].reshape(1, length * rows)
    all_positive = facts[:, 1].reshape(1, length * rows).astype(jnp.int32)

    column = jnp.arange(length * rows, dtype=jnp.int32)[None, :]
    target = (positive[:, None] == column).astype(jnp.float32)
    grad_block = (exp_scores / total[:, None] - target).astype(bf16)

    own_row = me_blk * rows + jnp.arange(rows, dtype=jnp.int32)[:, None]
    exp_back = jnp.exp(dot(p_half, q_group, 1, 1) / TAU)
    back_target = (all_positive == own_row).astype(jnp.float32)
    grad_back = (exp_back / all_total - back_target).astype(bf16)
    picked = jnp.where(names, got_weights, 0.0).astype(bf16)
    p_dir = (dot(grad_back, q_group, 1, 0) + dot(picked, got_q, 1, 0)) / TAU

    q_dir = (dot(grad_block, p_group, 1, 0) + dot(weights, got_p, 1, 0)) / TAU
    return (tangent(q_unit, q_scale, q_dir), tangent(p_unit, p_scale, p_dir))


def solution(mesh):
    return jax.shard_map(
        local,
        mesh=mesh,
        in_specs=(
            P(("blk", "dp"), None),
            P(("blk", "dp"), None),
            P(("blk", "dp")),
            P(("blk", "dp"), None),
            P(("blk", "dp")),
        ),
        out_specs=(P(("blk", "dp"), None), P(("blk", "dp"), None)),
        check_vma=False,
    )
```

```python
import jax
import jax.numpy as jnp
from jax import lax
from jax.sharding import PartitionSpec as P

EPS = 1e-06
TAU = 0.02


def unit_rows(x):
    xf = x.astype(jnp.float32)
    scale = lax.rsqrt(jnp.sum(xf * xf, axis=1, keepdims=True) + EPS)
    return (xf * scale, scale)


def tangent(unit, scale, direction):
    along = jnp.sum(unit * direction, axis=1, keepdims=True)
    return (scale * (direction - unit * along)).astype(jnp.bfloat16)


def dot(a, b, ca, cb):
    return lax.dot_general(a, b, (((ca,), (cb,)), ((), ())), preferred_element_type=jnp.float32)


def exchange(value, axis):
    return lax.all_to_all(value, axis, split_axis=0, concat_axis=0, tiled=True)


def local(queries, passages, positive, hard_ids, hard_count):
    rows, width = queries.shape
    hmax = hard_ids.shape[1]
    length = lax.axis_size("blk")
    peers = lax.axis_size("dp")
    me_blk = lax.axis_index("blk")
    me_dp = lax.axis_index("dp")
    limit = 2 * rows * hmax // peers
    slots = peers * limit
    entries = rows * hmax
    bf16 = jnp.bfloat16

    own_ids = hard_ids.T.reshape(entries)
    all_ids = exchange(jnp.broadcast_to(own_ids[None, :], (peers, entries)), "dp")

    p_unit, p_scale = unit_rows(passages)
    p_half = p_unit.astype(bf16)
    p_group = lax.all_gather(p_half, "blk", axis=0, tiled=True)
    q_unit, q_scale = unit_rows(queries)
    q_half = q_unit.astype(bf16)
    q_group = lax.all_gather(q_half, "blk", axis=0, tiled=True)

    number = jnp.arange(entries, dtype=jnp.int32)
    mine = all_ids // rows == me_dp
    earlier = (number[:, None] < number[None, :]).astype(bf16)
    mine_rank = dot(mine.astype(bf16), earlier, 1, 0).astype(jnp.int32)
    mine_rank = jnp.where(mine, mine_rank, -1)
    in_slot = mine_rank[:, None, :] == jnp.arange(limit, dtype=jnp.int32)[None, :, None]
    asked = jnp.sum(jnp.where(in_slot, (all_ids % rows + 1)[:, None, :], 0), axis=2) - 1
    names = asked.reshape(1, slots) == jnp.arange(rows, dtype=jnp.int32)[:, None]

    sent_p = dot(names.astype(bf16), p_half, 0, 0).astype(bf16)
    got_p = exchange(sent_p.reshape(peers, limit, width), "dp").reshape(slots, width)

    owner = own_ids // rows
    before = (owner[:, None] == owner[None, :]) & (number[None, :] < number[:, None])
    rank = jnp.sum(before.astype(jnp.int32), axis=1)
    place = (owner * limit + rank).reshape(hmax, rows)
    used = jnp.arange(hmax, dtype=jnp.int32)[:, None] < hard_count[None, :]
    used_place = jnp.where(used, place, -1)
    slot = jnp.arange(slots, dtype=jnp.int32)
    weighs = jnp.any(used_place[:, :, None] == slot[None, None, :], axis=0)

    scores = dot(q_half, p_group, 1, 1) / TAU
    exp_scores = jnp.exp(scores)
    hard_scores = dot(q_half, got_p, 1, 1) / TAU
    exp_hard = jnp.where(weighs, jnp.exp(hard_scores), 0.0)
    total = jnp.sum(exp_scores, axis=1) + jnp.sum(exp_hard, axis=1)
    weights = (exp_hard / total[:, None]).astype(bf16)

    sent_q = (dot(weights, q_half, 0, 0) / TAU).astype(bf16)
    got_q = exchange(sent_q.reshape(peers, limit, width), "dp").reshape(slots, width)

    facts = jnp.stack([total, positive.astype(jnp.float32)])
    facts = exchange(jnp.broadcast_to(facts[None], (length, 2, rows)), "blk")
    all_total = facts[:, 0].reshape(1, length * rows)
    all_positive = facts[:, 1].reshape(1, length * rows).astype(jnp.int32)

    column = jnp.arange(length * rows, dtype=jnp.int32)[None, :]
    target = (positive[:, None] == column).astype(jnp.float32)
    grad_block = (exp_scores / total[:, None] - target).astype(bf16)
    q_dir = (dot(grad_block, p_group, 1, 0) + dot(weights, got_p, 1, 0)) / TAU

    own_row = me_blk * rows + jnp.arange(rows, dtype=jnp.int32)[:, None]
    exp_back = jnp.exp(dot(p_half, q_group, 1, 1) / TAU)
    back_target = (all_positive == own_row).astype(jnp.float32)
    grad_back = (exp_back / all_total - back_target).astype(bf16)
    group_term = dot(grad_back, q_group, 1, 0) / TAU
    p_dir = group_term + dot(names.astype(bf16), got_q, 1, 0)

    return (tangent(q_unit, q_scale, q_dir), tangent(p_unit, p_scale, p_dir))


def solution(mesh):
    return jax.shard_map(
        local,
        mesh=mesh,
        in_specs=(
            P(("blk", "dp"), None),
            P(("blk", "dp"), None),
            P(("blk", "dp")),
            P(("blk", "dp"), None),
            P(("blk", "dp")),
        ),
        out_specs=(P(("blk", "dp"), None), P(("blk", "dp"), None)),
        check_vma=False,
    )
```

```python
import jax
import jax.numpy as jnp
from jax import lax
from jax.sharding import PartitionSpec as P

EPS = 1e-06
TAU = 0.02


def unit_rows(x):
    xf = x.astype(jnp.float32)
    scale = lax.rsqrt(jnp.sum(xf * xf, axis=1, keepdims=True) + EPS)
    return (xf * scale, scale)


def tangent(unit, scale, direction):
    along = jnp.sum(unit * direction, axis=1, keepdims=True)
    return (scale * (direction - unit * along)).astype(jnp.bfloat16)


def dot(a, b, ca, cb):
    return lax.dot_general(a, b, (((ca,), (cb,)), ((), ())), preferred_element_type=jnp.float32)


def exchange(value, axis):
    return lax.all_to_all(value, axis, split_axis=0, concat_axis=0, tiled=True)


def shifted(value, axis, move):
    devices = lax.axis_size(axis)
    return lax.ppermute(value, axis, [(i, move(i)) for i in range(devices)])


def gather_blk(value, me):
    length = lax.axis_size("blk")
    half = length // 2
    chips = half // 2

    def beside(i, step):
        return i // half * half + (i % half // 2 + step) % chips * 2 + i % 2

    pair = jnp.stack([value, shifted(value, "blk", lambda i: (i + half) % length)], axis=1)
    around = [pair]
    around += [shifted(pair, "blk", lambda i, s=s: beside(i, s)) for s in range(1, chips)]
    around = jnp.stack(around, axis=1)
    parts = []
    for k in range(value.shape[0]):
        other = shifted(around[k], "blk", lambda i: i // 2 * 2 + 1 - i % 2)
        parts.append(jnp.stack([around[k], other]).reshape(-1, value.shape[-1]))
    where = []
    for core in range(2):
        for step in range(chips):
            for z in range(2):
                there = beside((me + half * z) % length, chips - step)
                where.append(there // 2 * 2 + (there + core) % 2)
    return parts, jnp.stack(where)


def local(queries, passages, positive, hard_ids, hard_count):
    rows, width = queries.shape
    hmax = hard_ids.shape[1]
    length = lax.axis_size("blk")
    peers = lax.axis_size("dp")
    me_blk = lax.axis_index("blk")
    me_dp = lax.axis_index("dp")
    limit = 2 * rows * hmax // peers
    slots = peers * limit
    entries = rows * hmax
    bf16 = jnp.bfloat16

    own_ids = hard_ids.T.reshape(entries)
    all_ids = exchange(jnp.broadcast_to(own_ids[None, :], (peers, entries)), "dp")

    p_unit, p_scale = unit_rows(passages)
    p_half = p_unit.astype(bf16)
    q_unit, q_scale = unit_rows(queries)
    q_half = q_unit.astype(bf16)
    (p_group, q_group), where = gather_blk(jnp.stack([p_half, q_half]), me_blk)

    number = jnp.arange(entries, dtype=jnp.int32)
    mine = all_ids // rows == me_dp
    earlier = (number[:, None] < number[None, :]).astype(bf16)
    mine_rank = dot(mine.astype(bf16), earlier, 1, 0).astype(jnp.int32)
    mine_rank = jnp.where(mine, mine_rank, -1)
    in_slot = mine_rank[:, None, :] == jnp.arange(limit, dtype=jnp.int32)[None, :, None]
    asked = jnp.sum(jnp.where(in_slot, (all_ids % rows + 1)[:, None, :], 0), axis=2) - 1
    names = asked.reshape(1, slots) == jnp.arange(rows, dtype=jnp.int32)[:, None]

    sent_p = dot(names.astype(bf16), p_half, 0, 0).astype(bf16)
    got_p = exchange(sent_p.reshape(peers, limit, width), "dp").reshape(slots, width)

    owner = own_ids // rows
    before = (owner[:, None] == owner[None, :]) & (number[None, :] < number[:, None])
    rank = jnp.sum(before.astype(jnp.int32), axis=1)
    place = (owner * limit + rank).reshape(hmax, rows)
    used = jnp.arange(hmax, dtype=jnp.int32)[:, None] < hard_count[None, :]
    used_place = jnp.where(used, place, -1)
    slot = jnp.arange(slots, dtype=jnp.int32)
    weighs = jnp.any(used_place[:, :, None] == slot[None, None, :], axis=0)

    scores = dot(q_half, p_group, 1, 1) / TAU
    exp_scores = jnp.exp(scores)
    hard_scores = dot(q_half, got_p, 1, 1) / TAU
    exp_hard = jnp.where(weighs, jnp.exp(hard_scores), 0.0)
    total = jnp.sum(exp_scores, axis=1) + jnp.sum(exp_hard, axis=1)
    weights = (exp_hard / total[:, None]).astype(bf16)

    sent_q = (dot(weights, q_half, 0, 0) / TAU).astype(bf16)
    got_q = exchange(sent_q.reshape(peers, limit, width), "dp").reshape(slots, width)

    facts = jnp.stack([total, positive.astype(jnp.float32)])
    facts = exchange(jnp.broadcast_to(facts[None], (length, 2, rows)), "blk")[where]
    all_total = facts[:, 0].reshape(1, length * rows)
    all_positive = facts[:, 1].reshape(1, length * rows).astype(jnp.int32)

    row = jnp.arange(rows, dtype=jnp.int32)
    column = (where[:, None] * rows + row[None, :]).reshape(1, length * rows)
    target = (positive[:, None] == column).astype(jnp.float32)
    grad_block = (exp_scores / total[:, None] - target).astype(bf16)
    q_dir = (dot(grad_block, p_group, 1, 0) + dot(weights, got_p, 1, 0)) / TAU

    own_row = me_blk * rows + row[:, None]
    exp_back = jnp.exp(dot(p_half, q_group, 1, 1) / TAU)
    back_target = (all_positive == own_row).astype(jnp.float32)
    grad_back = (exp_back / all_total - back_target).astype(bf16)
    group_term = dot(grad_back, q_group, 1, 0) / TAU
    p_dir = group_term + dot(names.astype(bf16), got_q, 1, 0)

    return (tangent(q_unit, q_scale, q_dir), tangent(p_unit, p_scale, p_dir))


def solution(mesh):
    return jax.shard_map(
        local,
        mesh=mesh,
        in_specs=(
            P(("blk", "dp"), None),
            P(("blk", "dp"), None),
            P(("blk", "dp")),
            P(("blk", "dp"), None),
            P(("blk", "dp")),
        ),
        out_specs=(P(("blk", "dp"), None), P(("blk", "dp"), None)),
        check_vma=False,
    )
```

```python
import jax
import jax.numpy as jnp
from jax import lax
from jax.sharding import PartitionSpec as P

EPS = 1e-06
TAU = 0.02


def unit_rows(x):
    xf = x.astype(jnp.float32)
    scale = lax.rsqrt(jnp.sum(xf * xf, axis=1, keepdims=True) + EPS)
    return (xf * scale, scale)


def tangent(unit, scale, direction):
    along = jnp.sum(unit * direction, axis=1, keepdims=True)
    return (scale * (direction - unit * along)).astype(jnp.bfloat16)


def dot(a, b, ca, cb):
    return lax.dot_general(a, b, (((ca,), (cb,)), ((), ())), preferred_element_type=jnp.float32)


def exchange(value, axis):
    return lax.all_to_all(value, axis, split_axis=0, concat_axis=0, tiled=True)


def shifted(value, axis, move):
    devices = lax.axis_size(axis)
    return lax.ppermute(value, axis, [(i, move(i)) for i in range(devices)])


def gather_blk(value, me):
    length = lax.axis_size("blk")
    half = length // 2
    chips = half // 2

    def beside(i, step):
        return i // half * half + (i % half // 2 + step) % chips * 2 + i % 2

    pair = jnp.stack([value, shifted(value, "blk", lambda i: (i + half) % length)], axis=1)
    around = [pair]
    around += [shifted(pair, "blk", lambda i, s=s: beside(i, s)) for s in range(1, chips)]
    around = jnp.stack(around, axis=1)
    parts = []
    for k in range(value.shape[0]):
        other = shifted(around[k], "blk", lambda i: i // 2 * 2 + 1 - i % 2)
        parts.append(jnp.stack([around[k], other]).reshape(-1, value.shape[-1]))
    where = []
    for core in range(2):
        for step in range(chips):
            for z in range(2):
                there = beside((me + half * z) % length, chips - step)
                where.append(there // 2 * 2 + (there + core) % 2)
    return parts, jnp.stack(where)


def local(queries, passages, positive, hard_ids, hard_count):
    rows, width = queries.shape
    hmax = hard_ids.shape[1]
    length = lax.axis_size("blk")
    peers = lax.axis_size("dp")
    me_blk = lax.axis_index("blk")
    me_dp = lax.axis_index("dp")
    nz = 4
    ny = peers // nz
    me_z = me_dp // ny
    me_y = me_dp % ny
    limit = 2 * rows * hmax // peers
    slots = peers * limit
    entries = rows * hmax
    bf16 = jnp.bfloat16

    own_ids = hard_ids.T.reshape(entries)
    all_ids = exchange(jnp.broadcast_to(own_ids[None, :], (peers, entries)), "dp")

    q_unit, q_scale = unit_rows(queries)
    q_half = q_unit.astype(bf16)
    p_unit, p_scale = unit_rows(passages)
    p_half = p_unit.astype(bf16)

    lines = [[z * ny + y for y in range(ny)] for z in range(nz)]
    q_line = lax.all_gather(q_half, "dp", axis=0, tiled=True, axis_index_groups=lines)

    def along_z(i, step):
        return (i + step * ny) % peers

    def along_y(i, step):
        return i // ny * ny + (i + step) % ny

    p_line = [p_half]
    p_line += [shifted(p_half, "dp", lambda i, t=t: along_z(i, -t)) for t in range(1, nz)]
    p_line = jnp.concatenate(p_line)

    (p_group, q_group), where = gather_blk(jnp.stack([p_half, q_half]), me_blk)

    number = jnp.arange(entries, dtype=jnp.int32)
    ranks = jnp.arange(limit, dtype=jnp.int32)
    turn = jnp.arange(nz, dtype=jnp.int32)
    earlier = (number[:, None] < number[None, :]).astype(bf16)

    def find(ids, owners, value):
        mine = ids // rows == owners
        count = dot(mine.astype(bf16).reshape(-1, entries), earlier, 1, 0).astype(jnp.int32)
        rank = jnp.where(mine, count.reshape(mine.shape), -1)
        hit = rank[..., None, :] == ranks[:, None]
        return jnp.sum(jnp.where(hit, value[..., None, :], 0), axis=-1)

    line_ids = lax.dynamic_slice_in_dim(all_ids, me_z * ny, ny, 0)
    coded = (line_ids % rows + 1) * (2 * rows) + (number % rows + 1)[None, :]
    owners = ((me_z + turn) % nz * ny + me_y)[:, None, None]
    table = find(line_ids[None], owners, coded[None])
    asked_row = table // (2 * rows) - 1
    asked_by = table % (2 * rows) - 1

    index = jnp.where(asked_row >= 0, turn[:, None, None] * rows + asked_row, -1)
    index = jnp.swapaxes(index, 0, 1)
    index = lax.dynamic_slice_in_dim(jnp.concatenate([index, index]), me_y, ny, 0)
    pick = index.reshape(1, slots) == jnp.arange(nz * rows, dtype=jnp.int32)[:, None]
    sent_p = dot(pick.astype(bf16), p_line, 0, 0).astype(bf16).reshape(ny, slots // ny, width)
    got_p = [sent_p[0]]
    got_p += [shifted(sent_p[s], "dp", lambda i, s=s: along_y(i, s)) for s in range(1, ny)]
    got_p = jnp.concatenate(got_p)

    index = jnp.arange(ny, dtype=jnp.int32)[None, :, None] * rows + asked_by
    index = jnp.where(asked_by >= 0, index, -1)
    pick = index.reshape(1, slots) == jnp.arange(ny * rows, dtype=jnp.int32)[:, None]
    sent_q = dot(pick.astype(bf16), q_line, 0, 0).astype(bf16).reshape(nz, slots // nz, width)
    got_q = [sent_q[0]]
    got_q += [shifted(sent_q[t], "dp", lambda i, t=t: along_z(i, t)) for t in range(1, nz)]
    got_q = jnp.concatenate(got_q)

    asked = find(all_ids, me_dp, all_ids % rows + 1) - 1
    from_z = ((me_z - turn) % nz)[:, None] == turn[None, :]

    def by_turn(value):
        value = value.reshape(1, nz, slots // nz)
        return jnp.sum(jnp.where(from_z[:, :, None], value, 0), axis=1).reshape(1, slots)

    names = by_turn(asked) == jnp.arange(rows, dtype=jnp.int32)[:, None]

    owner = own_ids // rows
    before = (owner[:, None] == owner[None, :]) & (number[None, :] < number[:, None])
    rank = jnp.sum(before.astype(jnp.int32), axis=1)
    step = (me_y - owner) % ny * nz + (owner // ny - me_z) % nz
    place = (step * limit + rank).reshape(hmax, rows)
    used = jnp.arange(hmax, dtype=jnp.int32)[:, None] < hard_count[None, :]
    used_place = jnp.where(used, place, -1)
    slot = jnp.arange(slots, dtype=jnp.int32)
    weighs = jnp.any(used_place[:, :, None] == slot[None, None, :], axis=0)

    scores = dot(q_half, p_group, 1, 1) / TAU
    exp_scores = jnp.exp(scores)
    hard_scores = dot(q_half, got_p, 1, 1) / TAU
    exp_hard = jnp.where(weighs, jnp.exp(hard_scores), 0.0)
    total = jnp.sum(exp_scores, axis=1) + jnp.sum(exp_hard, axis=1)
    weights = (exp_hard / total[:, None]).astype(bf16)

    peer = jnp.arange(peers, dtype=jnp.int32)
    step = (me_y - peer) % ny * nz + (peer // ny - me_z) % nz
    slot_weights = jnp.sum(weights.astype(jnp.float32), axis=0).reshape(1, peers, limit)
    slot_weights = jnp.sum(
        jnp.where(step[:, None, None] == peer[None, :, None], slot_weights, 0.0), axis=1
    )
    got_weights = exchange(slot_weights, "dp")
    facts = jnp.stack([total, positive.astype(jnp.float32)])
    facts = exchange(jnp.broadcast_to(facts[None], (length, 2, rows)), "blk")[where]
    all_total = facts[:, 0].reshape(1, length * rows)
    all_positive = facts[:, 1].reshape(1, length * rows).astype(jnp.int32)

    row = jnp.arange(rows, dtype=jnp.int32)
    column = (where[:, None] * rows + row[None, :]).reshape(1, length * rows)
    target = (positive[:, None] == column).astype(jnp.float32)
    grad_block = (exp_scores / total[:, None] - target).astype(bf16)
    q_dir = (dot(grad_block, p_group, 1, 0) + dot(weights, got_p, 1, 0)) / TAU

    own_row = me_blk * rows + row[:, None]
    exp_back = jnp.exp(dot(p_half, q_group, 1, 1) / TAU)
    back_target = (all_positive == own_row).astype(jnp.float32)
    grad_back = (exp_back / all_total - back_target).astype(bf16)
    hard_back = jnp.where(names, by_turn(got_weights), 0.0).astype(bf16)
    p_dir = (dot(grad_back, q_group, 1, 0) + dot(hard_back, got_q, 1, 0)) / TAU

    return (tangent(q_unit, q_scale, q_dir), tangent(p_unit, p_scale, p_dir))


def solution(mesh):
    return jax.shard_map(
        local,
        mesh=mesh,
        in_specs=(
            P(("blk", "dp"), None),
            P(("blk", "dp"), None),
            P(("blk", "dp")),
            P(("blk", "dp"), None),
            P(("blk", "dp")),
        ),
        out_specs=(P(("blk", "dp"), None), P(("blk", "dp"), None)),
        check_vma=False,
    )
```

```python
import jax
import jax.numpy as jnp
from jax import lax
from jax.experimental import pallas as pl
from jax.experimental.pallas import tpu as pltpu
from jax.sharding import PartitionSpec as P

EPS = 1e-06
TAU = 0.02


def unit_rows(x):
    xf = x.astype(jnp.float32)
    scale = lax.rsqrt(jnp.sum(xf * xf, axis=1, keepdims=True) + EPS)
    return (xf * scale, scale)


def unit_kernel(q_ref, p_ref, q_half, p_half, both, q_scale, p_scale):
    for at, x_ref, half, scale in ((0, p_ref, p_half, p_scale), (1, q_ref, q_half, q_scale)):
        unit, factor = unit_rows(x_ref[...])
        half[...] = unit.astype(jnp.bfloat16)
        both[at] = unit.astype(jnp.bfloat16)
        scale[...] = factor


def unit_halves(queries, passages):
    rows, width = queries.shape
    half = jax.ShapeDtypeStruct((rows, width), jnp.bfloat16)
    scale = jax.ShapeDtypeStruct((rows, 1), jnp.float32)
    return pl.pallas_call(
        unit_kernel,
        out_shape=(half, half, jax.ShapeDtypeStruct((2, rows, width), jnp.bfloat16), scale, scale),
        cost_estimate=pl.CostEstimate(
            flops=8 * rows * width, bytes_accessed=12 * rows * width, transcendentals=0
        ),
        name="unit_halves",
    )(queries, passages)


def pick_kernel(index_ref, pool_ref, out_ref):
    rows = pool_ref.shape[1]
    index = index_ref[0]
    pick = index == lax.broadcasted_iota(jnp.int32, (rows, index.shape[1]), 0)
    found = lax.dot_general(
        pick.astype(jnp.bfloat16),
        pool_ref[0],
        (((0,), (0,)), ((), ())),
        preferred_element_type=jnp.float32,
    )
    out_ref[...] = found.astype(jnp.bfloat16).reshape(out_ref.shape)


def pick_rows(index, pool):
    groups, rows, width = pool.shape
    _, parts, ranks = index.shape
    found = pl.pallas_call(
        pick_kernel,
        grid=(groups,),
        in_specs=[
            pl.BlockSpec((1, 1, parts * ranks), lambda g: (g, 0, 0)),
            pl.BlockSpec((1, rows, width), lambda g: (g, 0, 0)),
        ],
        out_specs=pl.BlockSpec((parts, 1, ranks, width), lambda g: (0, g, 0, 0)),
        out_shape=jax.ShapeDtypeStruct((parts, groups, ranks, width), jnp.bfloat16),
        compiler_params=pltpu.CompilerParams(vmem_limit_bytes=16 * 1024 * 1024),
        cost_estimate=pl.CostEstimate(
            flops=2 * groups * rows * parts * ranks * width,
            bytes_accessed=2 * groups * (rows + parts * ranks) * width,
            transcendentals=0,
        ),
        name="pick_rows",
    )(index.reshape(groups, 1, parts * ranks), pool)
    return found.reshape(parts, groups * ranks, width)


def tangent(unit, scale, direction):
    along = jnp.sum(unit * direction, axis=1, keepdims=True)
    return (scale * (direction - unit * along)).astype(jnp.bfloat16)


def dot(a, b, ca, cb):
    return lax.dot_general(a, b, (((ca,), (cb,)), ((), ())), preferred_element_type=jnp.float32)


def exchange(value, axis, groups=None):
    return lax.all_to_all(
        value, axis, split_axis=0, concat_axis=0, tiled=True, axis_index_groups=groups
    )


def shifted(value, axis, move):
    devices = lax.axis_size(axis)
    return lax.ppermute(value, axis, [(i, move(i)) for i in range(devices)])


def gather_blk(value, me):
    length = lax.axis_size("blk")
    half = length // 2
    chips = half // 2

    def beside(i, step):
        return i // half * half + (i % half // 2 + step) % chips * 2 + i % 2

    pair = jnp.stack([value, shifted(value, "blk", lambda i: (i + half) % length)], axis=1)
    around = [pair]
    around += [shifted(pair, "blk", lambda i, s=s: beside(i, s)) for s in range(1, chips)]
    around = jnp.stack(around, axis=1)
    parts = []
    for k in range(value.shape[0]):
        other = shifted(around[k], "blk", lambda i: i // 2 * 2 + 1 - i % 2)
        parts.append(jnp.stack([around[k], other]).reshape(-1, value.shape[-1]))
    where = []
    for core in range(2):
        for step in range(chips):
            for z in range(2):
                there = beside((me + half * z) % length, chips - step)
                where.append(there // 2 * 2 + (there + core) % 2)
    return parts, jnp.stack(where)


def local(queries, passages, positive, hard_ids, hard_count):
    rows, width = queries.shape
    hmax = hard_ids.shape[1]
    length = lax.axis_size("blk")
    peers = lax.axis_size("dp")
    me_blk = lax.axis_index("blk")
    me_dp = lax.axis_index("dp")
    nz = 4
    ny = peers // nz
    me_z = me_dp // ny
    me_y = me_dp % ny
    limit = 2 * rows * hmax // peers
    slots = peers * limit
    entries = rows * hmax
    bf16 = jnp.bfloat16

    own_ids = hard_ids.T.reshape(entries)
    all_ids = exchange(jnp.broadcast_to(own_ids[None, :], (peers, entries)), "dp")

    q_half, p_half, both, q_scale, p_scale = unit_halves(queries, passages)

    lines = [[z * ny + y for y in range(ny)] for z in range(nz)]
    q_line = lax.all_gather(q_half, "dp", axis=0, tiled=True, axis_index_groups=lines)

    def along_z(i, step):
        return (i + step * ny) % peers

    p_line = [p_half]
    p_line += [shifted(p_half, "dp", lambda i, t=t: along_z(i, -t)) for t in range(1, nz)]
    p_line = jnp.stack(p_line)

    (p_group, q_group), where = gather_blk(both, me_blk)

    number = jnp.arange(entries, dtype=jnp.int32)
    ranks = jnp.arange(limit, dtype=jnp.int32)
    turn = jnp.arange(nz, dtype=jnp.int32)
    earlier = (number[:, None] < number[None, :]).astype(bf16)

    def find(ids, owners, value):
        mine = ids // rows == owners
        count = dot(mine.astype(bf16).reshape(-1, entries), earlier, 1, 0).astype(jnp.int32)
        rank = jnp.where(mine, count.reshape(mine.shape), -1)
        hit = rank[..., None, :] == ranks[:, None]
        return jnp.sum(jnp.where(hit, value[..., None, :], 0), axis=-1)

    line_ids = lax.dynamic_slice_in_dim(all_ids, me_z * ny, ny, 0)
    coded = (line_ids % rows + 1) * (2 * rows) + (number % rows + 1)[None, :]
    owners = ((me_z + turn) % nz * ny + me_y)[:, None, None]
    table = find(line_ids[None], owners, coded[None])
    asked_row = table // (2 * rows) - 1
    asked_by = table % (2 * rows) - 1

    sent_p = pick_rows(asked_row, p_line)
    got_p = exchange(sent_p, "dp", lines).reshape(slots, width)

    sent_q = pick_rows(jnp.swapaxes(asked_by, 0, 1), q_line.reshape(ny, rows, width))
    got_q = [sent_q[0]]
    got_q += [shifted(sent_q[t], "dp", lambda i, t=t: along_z(i, t)) for t in range(1, nz)]
    got_q = jnp.concatenate(got_q)

    asked = find(all_ids, me_dp, all_ids % rows + 1) - 1
    from_z = ((me_z - turn) % nz)[:, None] == turn[None, :]

    def by_turn(value):
        value = value.reshape(1, nz, slots // nz)
        return jnp.sum(jnp.where(from_z[:, :, None], value, 0), axis=1).reshape(1, slots)

    names = by_turn(asked) == jnp.arange(rows, dtype=jnp.int32)[:, None]

    owner = own_ids // rows
    before = (owner[:, None] == owner[None, :]) & (number[None, :] < number[:, None])
    rank = jnp.sum(before.astype(jnp.int32), axis=1)
    step = owner % ny * nz + (owner // ny - me_z) % nz
    place = (step * limit + rank).reshape(hmax, rows)
    used = jnp.arange(hmax, dtype=jnp.int32)[:, None] < hard_count[None, :]
    used_place = jnp.where(used, place, -1)
    slot = jnp.arange(slots, dtype=jnp.int32)
    weighs = jnp.any(used_place[:, :, None] == slot[None, None, :], axis=0)

    scores = dot(q_half, p_group, 1, 1) / TAU
    exp_scores = jnp.exp(scores)
    hard_scores = dot(q_half, got_p, 1, 1) / TAU
    exp_hard = jnp.where(weighs, jnp.exp(hard_scores), 0.0)
    total = jnp.sum(exp_scores, axis=1) + jnp.sum(exp_hard, axis=1)
    weights = (exp_hard / total[:, None]).astype(bf16)

    peer = jnp.arange(peers, dtype=jnp.int32)
    step = peer % ny * nz + (peer // ny - me_z) % nz
    slot_weights = jnp.sum(weights.astype(jnp.float32), axis=0).reshape(1, peers, limit)
    slot_weights = jnp.sum(
        jnp.where(step[:, None, None] == peer[None, :, None], slot_weights, 0.0), axis=1
    )
    got_weights = exchange(slot_weights, "dp")
    facts = jnp.stack([total, positive.astype(jnp.float32)])
    facts = gather_blk(facts[None], me_blk)[0][0].reshape(length, 2, rows)
    all_total = facts[:, 0].reshape(1, length * rows)
    all_positive = facts[:, 1].reshape(1, length * rows).astype(jnp.int32)

    row = jnp.arange(rows, dtype=jnp.int32)
    column = (where[:, None] * rows + row[None, :]).reshape(1, length * rows)
    target = (positive[:, None] == column).astype(jnp.float32)
    grad_block = (exp_scores / total[:, None] - target).astype(bf16)
    q_dir = (dot(grad_block, p_group, 1, 0) + dot(weights, got_p, 1, 0)) / TAU

    own_row = me_blk * rows + row[:, None]
    exp_back = jnp.exp(dot(p_half, q_group, 1, 1) / TAU)
    back_target = (all_positive == own_row).astype(jnp.float32)
    grad_back = (exp_back / all_total - back_target).astype(bf16)
    hard_back = jnp.where(names, by_turn(got_weights), 0.0).astype(bf16)
    p_dir = (dot(grad_back, q_group, 1, 0) + dot(hard_back, got_q, 1, 0)) / TAU

    q_unit = queries.astype(jnp.float32) * q_scale
    p_unit = passages.astype(jnp.float32) * p_scale
    return (tangent(q_unit, q_scale, q_dir), tangent(p_unit, p_scale, p_dir))


def solution(mesh):
    return jax.shard_map(
        local,
        mesh=mesh,
        in_specs=(
            P(("blk", "dp"), None),
            P(("blk", "dp"), None),
            P(("blk", "dp")),
            P(("blk", "dp"), None),
            P(("blk", "dp")),
        ),
        out_specs=(P(("blk", "dp"), None), P(("blk", "dp"), None)),
        check_vma=False,
    )
```

```python
import jax
import jax.numpy as jnp
from jax import lax
from jax.experimental import pallas as pl
from jax.experimental.pallas import tpu as pltpu
from jax.sharding import PartitionSpec as P

EPS = 1e-06
TAU = 0.02


def unit_rows(x):
    xf = x.astype(jnp.float32)
    scale = lax.rsqrt(jnp.sum(xf * xf, axis=1, keepdims=True) + EPS)
    return (xf * scale, scale)


def unit_kernel(q_ref, p_ref, q_half, p_half, both, q_scale, p_scale):
    for at, x_ref, half, scale in ((0, p_ref, p_half, p_scale), (1, q_ref, q_half, q_scale)):
        unit, factor = unit_rows(x_ref[...])
        half[...] = unit.astype(jnp.bfloat16)
        both[at] = unit.astype(jnp.bfloat16)
        scale[...] = factor


def unit_halves(queries, passages):
    rows, width = queries.shape
    half = jax.ShapeDtypeStruct((rows, width), jnp.bfloat16)
    scale = jax.ShapeDtypeStruct((rows, 1), jnp.float32)
    return pl.pallas_call(
        unit_kernel,
        out_shape=(half, half, jax.ShapeDtypeStruct((2, rows, width), jnp.bfloat16), scale, scale),
        cost_estimate=pl.CostEstimate(
            flops=8 * rows * width, bytes_accessed=12 * rows * width, transcendentals=0
        ),
        name="unit_halves",
    )(queries, passages)


def pick_kernel(index_ref, pool_ref, out_ref):
    rows = pool_ref.shape[1]
    index = index_ref[0]
    pick = index == lax.broadcasted_iota(jnp.int32, (rows, index.shape[1]), 0)
    found = lax.dot_general(
        pick.astype(jnp.bfloat16),
        pool_ref[0],
        (((0,), (0,)), ((), ())),
        preferred_element_type=jnp.float32,
    )
    out_ref[...] = found.astype(jnp.bfloat16).reshape(out_ref.shape)


def pick_rows(index, pool):
    groups, rows, width = pool.shape
    _, parts, ranks = index.shape
    found = pl.pallas_call(
        pick_kernel,
        grid=(groups,),
        in_specs=[
            pl.BlockSpec((1, 1, parts * ranks), lambda g: (g, 0, 0)),
            pl.BlockSpec((1, rows, width), lambda g: (g, 0, 0)),
        ],
        out_specs=pl.BlockSpec((parts, 1, ranks, width), lambda g: (0, g, 0, 0)),
        out_shape=jax.ShapeDtypeStruct((parts, groups, ranks, width), jnp.bfloat16),
        compiler_params=pltpu.CompilerParams(vmem_limit_bytes=16 * 1024 * 1024),
        cost_estimate=pl.CostEstimate(
            flops=2 * groups * rows * parts * ranks * width,
            bytes_accessed=2 * groups * (rows + parts * ranks) * width,
            transcendentals=0,
        ),
        name="pick_rows",
    )(index.reshape(groups, 1, parts * ranks), pool)
    return found.reshape(parts, groups * ranks, width)


def tangent(unit, scale, direction):
    along = jnp.sum(unit * direction, axis=1, keepdims=True)
    return (scale * (direction - unit * along)).astype(jnp.bfloat16)


def dot(a, b, ca, cb):
    return lax.dot_general(a, b, (((ca,), (cb,)), ((), ())), preferred_element_type=jnp.float32)


def exchange(value, axis, groups=None):
    return lax.all_to_all(
        value, axis, split_axis=0, concat_axis=0, tiled=True, axis_index_groups=groups
    )


def shifted(value, axis, move):
    devices = lax.axis_size(axis)
    return lax.ppermute(value, axis, [(i, move(i)) for i in range(devices)])


def beside(i, step, length):
    half = length // 2
    return i // half * half + (i % half // 2 + step) % (half // 2) * 2 + i % 2


def sibling(i):
    return i // 2 * 2 + 1 - i % 2


def blk_order(me):
    length = lax.axis_size("blk")
    where = []
    for core in range(2):
        for step in range(length // 4):
            for z in range(2):
                there = beside((me + length // 2 * z) % length, -step, length)
                where.append(there // 2 * 2 + (there + core) % 2)
    return jnp.stack(where)


def gather_chips(both):
    length = lax.axis_size("blk")

    def turned(value, step):
        return shifted(value, "blk", lambda i: beside(i, step, length))

    over = shifted(both, "blk", lambda i: (i + length // 2) % length)
    pair = jnp.stack([both, over], axis=1)
    right = turned(pair, 1)
    left = turned(pair, -1)
    far = (turned(right[0], 1), turned(left[1], -1))
    return [jnp.stack([pair[k], right[k], far[k], left[k]]) for k in range(2)]


def both_cores(value, width):
    other = shifted(value, "blk", sibling)
    return jnp.stack([value, other]).reshape(-1, width)


def gather_facts(value):
    length = lax.axis_size("blk")
    pair = jnp.stack([value, shifted(value, "blk", lambda i: (i + length // 2) % length)])
    around = [pair]
    for step in range(1, length // 4):
        around.append(shifted(pair, "blk", lambda i, s=step: beside(i, s, length)))
    around = jnp.stack(around)
    other = shifted(around, "blk", sibling)
    return jnp.stack([around, other]).reshape(length, *value.shape)


def local(queries, passages, positive, hard_ids, hard_count):
    rows, width = queries.shape
    hmax = hard_ids.shape[1]
    length = lax.axis_size("blk")
    peers = lax.axis_size("dp")
    me_blk = lax.axis_index("blk")
    me_dp = lax.axis_index("dp")
    nz = 4
    ny = peers // nz
    me_z = me_dp // ny
    me_y = me_dp % ny
    limit = 2 * rows * hmax // peers
    slots = peers * limit
    entries = rows * hmax
    bf16 = jnp.bfloat16

    own_ids = hard_ids.T.reshape(entries)

    q_half, p_half, both, q_scale, p_scale = unit_halves(queries, passages)

    lines = [[z * ny + y for y in range(ny)] for z in range(nz)]
    line_ids = exchange(jnp.broadcast_to(own_ids[None, :], (ny, entries)), "dp", lines)
    q_line = lax.all_gather(q_half, "dp", axis=0, tiled=True, axis_index_groups=lines)

    def along_z(i, step):
        return (i + step * ny) % peers

    p_line = [p_half]
    p_line += [shifted(p_half, "dp", lambda i, t=t: along_z(i, -t)) for t in range(1, nz)]
    p_line = jnp.stack(p_line)

    p_chips, q_chips = gather_chips(both)
    where = blk_order(me_blk)

    number = jnp.arange(entries, dtype=jnp.int32)
    ranks = jnp.arange(limit, dtype=jnp.int32)
    turn = jnp.arange(nz, dtype=jnp.int32)
    earlier = (number[:, None] < number[None, :]).astype(bf16)

    coded = (line_ids % rows + 1) * (2 * rows) + (number % rows + 1)[None, :]
    owners = ((me_z + turn) % nz * ny + me_y)[:, None, None]
    mine = line_ids[None] // rows == owners
    count = dot(mine.astype(bf16).reshape(-1, entries), earlier, 1, 0).astype(jnp.int32)
    rank = jnp.where(mine, count.reshape(mine.shape), -1)
    hit = rank[:, :, None, :] == ranks[:, None]
    table = jnp.sum(jnp.where(hit, coded[None, :, None, :], 0), axis=-1)
    asked_row = table // (2 * rows) - 1
    asked_by = table % (2 * rows) - 1

    sent_p = pick_rows(asked_row, p_line)
    got_p = exchange(sent_p, "dp", lines).reshape(slots, width)

    sent_q = pick_rows(jnp.swapaxes(asked_by, 0, 1), q_line.reshape(ny, rows, width))
    got_q = [sent_q[0]]
    got_q += [shifted(sent_q[t], "dp", lambda i, t=t: along_z(i, t)) for t in range(1, nz)]
    got_q = jnp.concatenate(got_q)

    p_chips, q_chips, got_q = lax.optimization_barrier((p_chips, q_chips, got_q))
    p_group = both_cores(p_chips, width)
    q_group = both_cores(q_chips, width)

    owner = own_ids // rows
    before = (owner[:, None] == owner[None, :]) & (number[None, :] < number[:, None])
    rank = jnp.sum(before.astype(jnp.int32), axis=1)
    step = owner % ny * nz + (owner // ny - me_z) % nz
    place = (step * limit + rank).reshape(hmax, rows)
    used = jnp.arange(hmax, dtype=jnp.int32)[:, None] < hard_count[None, :]
    used_place = jnp.where(used, place, -1)
    slot = jnp.arange(slots, dtype=jnp.int32)
    weighs = jnp.any(used_place[:, :, None] == slot[None, None, :], axis=0)
    wanted = jnp.where(used, own_ids.reshape(hmax, rows) % rows, 0)[:, :, None]
    own_asked = jnp.sum(
        jnp.where(used_place[:, :, None] == slot[None, None, :], wanted, 0), axis=(0, 1)
    )

    scores = dot(q_half, p_group, 1, 1) / TAU
    exp_scores = jnp.exp(scores)
    hard_scores = dot(q_half, got_p, 1, 1) / TAU
    exp_hard = jnp.where(weighs, jnp.exp(hard_scores), 0.0)
    total = jnp.sum(exp_scores, axis=1) + jnp.sum(exp_hard, axis=1)
    exp_back = jnp.exp(dot(p_half, q_group, 1, 1) / TAU)
    total, exp_back = lax.optimization_barrier((total, exp_back))
    weights = (exp_hard / total[:, None]).astype(bf16)

    peer = jnp.arange(peers, dtype=jnp.int32)
    step_of = (me_z + peer % nz) % nz * ny + peer // nz
    slot_weights = jnp.sum(weights.astype(jnp.float32), axis=0)
    by_slot = jnp.stack([slot_weights, own_asked.astype(jnp.float32)]).reshape(2, 1, peers, limit)
    to_owner = peer[:, None] == step_of[None, :]
    by_owner = jnp.sum(jnp.where(to_owner[None, :, :, None], by_slot, 0.0), axis=2)
    got = exchange(jnp.swapaxes(by_owner, 0, 1), "dp")
    from_z = ((me_z - turn) % nz)[:, None] == turn[None, :]
    got = got.reshape(1, nz, ny, 2, limit)
    got = jnp.sum(jnp.where(from_z[:, :, None, None, None], got, 0.0), axis=1)
    got_weights = got[:, :, 0].reshape(1, slots)
    asked = got[:, :, 1].reshape(1, slots).astype(jnp.int32)
    names = asked == jnp.arange(rows, dtype=jnp.int32)[:, None]
    facts = gather_facts(jnp.stack([total, positive.astype(jnp.float32)]))
    all_total = facts[:, 0].reshape(1, length * rows)
    all_positive = facts[:, 1].reshape(1, length * rows).astype(jnp.int32)

    row = jnp.arange(rows, dtype=jnp.int32)
    column = (where[:, None] * rows + row[None, :]).reshape(1, length * rows)
    target = (positive[:, None] == column).astype(jnp.float32)
    grad_block = (exp_scores / total[:, None] - target).astype(bf16)
    q_dir = (dot(grad_block, p_group, 1, 0) + dot(weights, got_p, 1, 0)) / TAU

    own_row = me_blk * rows + row[:, None]
    back_target = (all_positive == own_row).astype(jnp.float32)
    grad_back = (exp_back / all_total - back_target).astype(bf16)
    hard_back = jnp.where(names, got_weights, 0.0).astype(bf16)
    p_dir = (dot(grad_back, q_group, 1, 0) + dot(hard_back, got_q, 1, 0)) / TAU

    q_unit = queries.astype(jnp.float32) * q_scale
    p_unit = passages.astype(jnp.float32) * p_scale
    return (tangent(q_unit, q_scale, q_dir), tangent(p_unit, p_scale, p_dir))


def solution(mesh):
    return jax.shard_map(
        local,
        mesh=mesh,
        in_specs=(
            P(("blk", "dp"), None),
            P(("blk", "dp"), None),
            P(("blk", "dp")),
            P(("blk", "dp"), None),
            P(("blk", "dp")),
        ),
        out_specs=(P(("blk", "dp"), None), P(("blk", "dp"), None)),
        check_vma=False,
    )
```

```python
import jax
import jax.numpy as jnp
from jax import lax
from jax.experimental import pallas as pl
from jax.experimental.pallas import tpu as pltpu
from jax.sharding import PartitionSpec as P

EPS = 1e-06
TAU = 0.02


def unit_rows(x):
    xf = x.astype(jnp.float32)
    scale = lax.rsqrt(jnp.sum(xf * xf, axis=1, keepdims=True) + EPS)
    return (xf * scale, scale)


def unit_kernel(q_ref, p_ref, q_half, p_half, both, q_scale, p_scale):
    for at, x_ref, half, scale in ((0, p_ref, p_half, p_scale), (1, q_ref, q_half, q_scale)):
        unit, factor = unit_rows(x_ref[...])
        half[...] = unit.astype(jnp.bfloat16)
        both[at] = unit.astype(jnp.bfloat16)
        scale[...] = factor


def unit_halves(queries, passages):
    rows, width = queries.shape
    half = jax.ShapeDtypeStruct((rows, width), jnp.bfloat16)
    scale = jax.ShapeDtypeStruct((rows, 1), jnp.float32)
    return pl.pallas_call(
        unit_kernel,
        out_shape=(half, half, jax.ShapeDtypeStruct((2, rows, width), jnp.bfloat16), scale, scale),
        cost_estimate=pl.CostEstimate(
            flops=8 * rows * width, bytes_accessed=12 * rows * width, transcendentals=0
        ),
        name="unit_halves",
    )(queries, passages)


def pick_kernel(index_ref, pool_ref, out_ref):
    rows = pool_ref.shape[1]
    index = index_ref[0]
    pick = index == lax.broadcasted_iota(jnp.int32, (rows, index.shape[1]), 0)
    found = lax.dot_general(
        pick.astype(jnp.bfloat16),
        pool_ref[0],
        (((0,), (0,)), ((), ())),
        preferred_element_type=jnp.float32,
    )
    out_ref[...] = found.astype(jnp.bfloat16).reshape(out_ref.shape)


def pick_rows(index, pool):
    groups, rows, width = pool.shape
    _, parts, ranks = index.shape
    found = pl.pallas_call(
        pick_kernel,
        grid=(groups,),
        in_specs=[
            pl.BlockSpec((1, 1, parts * ranks), lambda g: (g, 0, 0)),
            pl.BlockSpec((1, rows, width), lambda g: (g, 0, 0)),
        ],
        out_specs=pl.BlockSpec((parts, 1, ranks, width), lambda g: (0, g, 0, 0)),
        out_shape=jax.ShapeDtypeStruct((parts, groups, ranks, width), jnp.bfloat16),
        compiler_params=pltpu.CompilerParams(vmem_limit_bytes=16 * 1024 * 1024),
        cost_estimate=pl.CostEstimate(
            flops=2 * groups * rows * parts * ranks * width,
            bytes_accessed=2 * groups * (rows + parts * ranks) * width,
            transcendentals=0,
        ),
        name="pick_rows",
    )(index.reshape(groups, 1, parts * ranks), pool)
    return found.reshape(parts, groups * ranks, width)


BRIEF = pl.CostEstimate(flops=1000, bytes_accessed=1000, transcendentals=0)
ROOMY = pltpu.CompilerParams(vmem_limit_bytes=32 * 1024 * 1024)
TILE = 256


def exp_kernel(x_ref, own_ref, other_ref, exp_ref, sum_ref):
    half = own_ref.shape[0]
    x = x_ref[...]
    added = jnp.zeros(sum_ref.shape, jnp.float32)
    for at, rows_ref in ((0, own_ref), (half, other_ref)):
        for tile in range(0, half, TILE):
            exps = jnp.exp(dot(x, rows_ref[tile : tile + TILE], 1, 1) / TAU)
            exp_ref[:, at + tile : at + tile + TILE] = exps
            added += jnp.sum(exps, axis=1, keepdims=True)
    sum_ref[...] = added


def exp_scores_of(x, own, other):
    rows = x.shape[0]
    return pl.pallas_call(
        exp_kernel,
        out_shape=(
            jax.ShapeDtypeStruct((rows, 2 * own.shape[0]), jnp.float32),
            jax.ShapeDtypeStruct((rows, 1), jnp.float32),
        ),
        compiler_params=ROOMY,
        cost_estimate=BRIEF,
        name="exp_scores",
    )(x, own, other)


def total_kernel(q_ref, hard_ref, mask_ref, sum_ref, positive_ref, total_ref, w_ref, s_ref, facts_ref):
    rows = q_ref.shape[0]
    q = q_ref[...]
    exps = []
    total = sum_ref[...]
    for tile in range(0, hard_ref.shape[0], TILE):
        scores = dot(q, hard_ref[tile : tile + TILE], 1, 1) / TAU
        exps.append(jnp.where(mask_ref[:, tile : tile + TILE] > 0, jnp.exp(scores), 0.0))
        total += jnp.sum(exps[-1], axis=1, keepdims=True)
    total_ref[...] = total
    for number, exp_hard in enumerate(exps):
        tile = number * TILE
        weights = (exp_hard / total).astype(jnp.bfloat16)
        w_ref[:, tile : tile + TILE] = weights
        s_ref[:, tile : tile + TILE] = jnp.sum(weights.astype(jnp.float32), axis=0, keepdims=True)
    across = lax.broadcasted_iota(jnp.int32, (rows, rows), 0)
    down = lax.broadcasted_iota(jnp.int32, (rows, rows), 1)
    total_row = jnp.sum(jnp.where(across == down, total, 0.0), axis=0, keepdims=True)
    for device in range(facts_ref.shape[0]):
        facts_ref[device, 0:1] = total_row
        facts_ref[device, 1:2] = positive_ref[...].astype(jnp.float32)


def totals_of(q_half, hard_rows, mask, sums, positive, length):
    rows = q_half.shape[0]
    slots = hard_rows.shape[0]
    return pl.pallas_call(
        total_kernel,
        out_shape=(
            jax.ShapeDtypeStruct((rows, 1), jnp.float32),
            jax.ShapeDtypeStruct((rows, slots), jnp.bfloat16),
            jax.ShapeDtypeStruct((1, slots), jnp.float32),
            jax.ShapeDtypeStruct((length, 2, rows), jnp.float32),
        ),
        compiler_params=ROOMY,
        cost_estimate=BRIEF,
        name="totals",
    )(q_half, hard_rows, mask, sums, positive.reshape(1, rows))


def grad_kernel(exp_ref, total_ref, mark_ref, marks_ref, own, other, w_ref, hard, x_ref, scale_ref, out_ref):
    half = own.shape[0]
    width = x_ref.shape[1]
    target = (mark_ref[...] == marks_ref[...]).astype(jnp.float32)
    grads = (exp_ref[...] / total_ref[...] - target).astype(jnp.bfloat16)
    weights = w_ref[...]
    scale = scale_ref[...]
    directions = []
    along = jnp.zeros(scale.shape, jnp.float32)
    for tile in range(0, width, TILE):
        cols = slice(tile, tile + TILE)
        direction = dot(grads[:, :half], own[:, cols], 1, 0) + dot(grads[:, half:], other[:, cols], 1, 0)
        direction = (direction + dot(weights, hard[:, cols], 1, 0)) / TAU
        unit = x_ref[:, cols].astype(jnp.float32) * scale
        along += jnp.sum(unit * direction, axis=1, keepdims=True)
        directions.append(direction)
    for number, direction in enumerate(directions):
        cols = slice(number * TILE, (number + 1) * TILE)
        unit = x_ref[:, cols].astype(jnp.float32) * scale
        out_ref[:, cols] = (scale * (direction - unit * along)).astype(jnp.bfloat16)


def grads_of(exps, total, mark, marks, own, other, weights, hard, x, scale):
    return pl.pallas_call(
        grad_kernel,
        out_shape=jax.ShapeDtypeStruct(x.shape, jnp.bfloat16),
        compiler_params=ROOMY,
        cost_estimate=BRIEF,
        name="gradients",
    )(exps, total, mark, marks, own, other, weights, hard, x, scale)


def dot(a, b, ca, cb):
    return lax.dot_general(a, b, (((ca,), (cb,)), ((), ())), preferred_element_type=jnp.float32)


def exchange(value, axis, groups=None):
    return lax.all_to_all(
        value, axis, split_axis=0, concat_axis=0, tiled=True, axis_index_groups=groups
    )


def shifted(value, axis, move):
    devices = lax.axis_size(axis)
    return lax.ppermute(value, axis, [(i, move(i)) for i in range(devices)])


def beside(i, step, length):
    half = length // 2
    return i // half * half + (i % half // 2 + step) % (half // 2) * 2 + i % 2


def sibling(i):
    return i // 2 * 2 + 1 - i % 2


def blk_order(me):
    length = lax.axis_size("blk")
    where = []
    for core in range(2):
        for step in range(length // 4):
            for z in range(2):
                there = beside((me + length // 2 * z) % length, -step, length)
                where.append(there // 2 * 2 + (there + core) % 2)
    return jnp.stack(where)


def gather_chips(both, after):
    length = lax.axis_size("blk")

    def turned(value, step):
        return shifted(value, "blk", lambda i: beside(i, step, length))

    over = shifted(both, "blk", lambda i: (i + length // 2) % length)
    pair = jnp.stack([both, over], axis=1)
    right = turned(pair, 1)
    left = turned(pair, -1)
    right, left, after = lax.optimization_barrier((right, left, after))
    far = (turned(right[0], 1), turned(left[1], -1))
    chips = [jnp.stack([pair[k], right[k], far[k], left[k]]) for k in range(2)]
    return [chip.reshape(-1, both.shape[2]) for chip in chips], after


def local(queries, passages, positive, hard_ids, hard_count):
    rows, width = queries.shape
    hmax = hard_ids.shape[1]
    length = lax.axis_size("blk")
    peers = lax.axis_size("dp")
    me_blk = lax.axis_index("blk")
    me_dp = lax.axis_index("dp")
    nz = 4
    ny = peers // nz
    me_z = me_dp // ny
    me_y = me_dp % ny
    limit = 2 * rows * hmax // peers
    slots = peers * limit
    entries = rows * hmax
    bf16 = jnp.bfloat16

    own_ids = hard_ids.T.reshape(entries)

    q_half, p_half, both, q_scale, p_scale = unit_halves(queries, passages)

    lines = [[z * ny + y for y in range(ny)] for z in range(nz)]
    line_ids = exchange(jnp.broadcast_to(own_ids[None, :], (ny, entries)), "dp", lines)
    q_line = lax.all_gather(q_half, "dp", axis=0, tiled=True, axis_index_groups=lines)

    def along_z(i, step):
        return (i + step * ny) % peers

    p_line = [p_half]
    p_line += [shifted(p_half, "dp", lambda i, t=t: along_z(i, -t)) for t in range(1, nz)]
    p_line = jnp.stack(p_line)

    number = jnp.arange(entries, dtype=jnp.int32)
    ranks = jnp.arange(limit, dtype=jnp.int32)
    turn = jnp.arange(nz, dtype=jnp.int32)
    earlier = (number[:, None] < number[None, :]).astype(bf16)

    coded = (line_ids % rows + 1) * (2 * rows) + (number % rows + 1)[None, :]
    owners = ((me_z + turn) % nz * ny + me_y)[:, None, None]
    mine = line_ids[None] // rows == owners
    count = dot(mine.astype(bf16).reshape(-1, entries), earlier, 1, 0).astype(jnp.int32)
    rank = jnp.where(mine, count.reshape(mine.shape), -1)
    hit = rank[:, :, None, :] == ranks[:, None]
    table = jnp.sum(jnp.where(hit, coded[None, :, None, :], 0), axis=-1)
    asked_row = table // (2 * rows) - 1
    asked_by = table % (2 * rows) - 1

    sent_p = pick_rows(asked_row, p_line)
    got_p = exchange(sent_p, "dp", lines).reshape(slots, width)

    sent_q = pick_rows(jnp.swapaxes(asked_by, 0, 1), q_line.reshape(ny, rows, width))
    (p_own, q_own), sent_q = gather_chips(both, sent_q)
    got_q = [sent_q[0]]
    got_q += [shifted(sent_q[t], "dp", lambda i, t=t: along_z(i, t)) for t in range(1, nz)]
    got_q = jnp.concatenate(got_q)

    p_other = shifted(p_own, "blk", sibling)
    q_other = shifted(q_own, "blk", sibling)
    where = blk_order(me_blk)

    owner = own_ids // rows
    before = (owner[:, None] == owner[None, :]) & (number[None, :] < number[:, None])
    rank = jnp.sum(before.astype(jnp.int32), axis=1)
    step = owner % ny * nz + (owner // ny - me_z) % nz
    place = (step * limit + rank).reshape(hmax, rows)
    used = jnp.arange(hmax, dtype=jnp.int32)[:, None] < hard_count[None, :]
    used_place = jnp.where(used, place, -1)
    slot = jnp.arange(slots, dtype=jnp.int32)
    weighs = jnp.any(used_place[:, :, None] == slot[None, None, :], axis=0)
    wanted = jnp.where(used, own_ids.reshape(hmax, rows) % rows, 0)[:, :, None]
    own_asked = jnp.sum(
        jnp.where(used_place[:, :, None] == slot[None, None, :], wanted, 0), axis=(0, 1)
    )

    exp_scores, sums = exp_scores_of(q_half, p_own, p_other)
    exp_back, _ = exp_scores_of(p_half, q_own, q_other)
    total, weights, slot_weights, facts = totals_of(
        q_half, got_p, weighs.astype(jnp.float32), sums, positive, length
    )

    peer = jnp.arange(peers, dtype=jnp.int32)
    step_of = (me_z + peer % nz) % nz * ny + peer // nz
    by_slot = jnp.stack([slot_weights[0], own_asked.astype(jnp.float32)])
    by_slot = by_slot.reshape(2, 1, peers, limit)
    to_owner = peer[:, None] == step_of[None, :]
    by_owner = jnp.sum(jnp.where(to_owner[None, :, :, None], by_slot, 0.0), axis=2)
    got = exchange(jnp.swapaxes(by_owner, 0, 1), "dp")
    from_z = ((me_z - turn) % nz)[:, None] == turn[None, :]
    got = got.reshape(1, nz, ny, 2, limit)
    got = jnp.sum(jnp.where(from_z[:, :, None, None, None], got, 0.0), axis=1)
    got_weights = got[:, :, 0].reshape(1, slots)
    asked = got[:, :, 1].reshape(1, slots).astype(jnp.int32)
    names = asked == jnp.arange(rows, dtype=jnp.int32)[:, None]
    hard_back = jnp.where(names, got_weights, 0.0).astype(bf16)
    facts = exchange(facts, "blk")[where]
    all_total = facts[:, 0].reshape(1, length * rows)
    all_positive = facts[:, 1].reshape(1, length * rows).astype(jnp.int32)

    row = jnp.arange(rows, dtype=jnp.int32)
    column = (where[:, None] * rows + row[None, :]).reshape(1, length * rows)
    own_row = me_blk * rows + row[:, None]
    query_grads = grads_of(
        exp_scores, total, positive[:, None], column,
        p_own, p_other, weights, got_p, queries, q_scale,
    )
    passage_grads = grads_of(
        exp_back, all_total, own_row, all_positive,
        q_own, q_other, hard_back, got_q, passages, p_scale,
    )
    return (query_grads, passage_grads)


def solution(mesh):
    return jax.shard_map(
        local,
        mesh=mesh,
        in_specs=(
            P(("blk", "dp"), None),
            P(("blk", "dp"), None),
            P(("blk", "dp")),
            P(("blk", "dp"), None),
            P(("blk", "dp")),
        ),
        out_specs=(P(("blk", "dp"), None), P(("blk", "dp"), None)),
        check_vma=False,
    )
```

```python
import jax
import jax.numpy as jnp
from jax import lax
from jax.experimental import pallas as pl
from jax.experimental.pallas import tpu as pltpu
from jax.sharding import PartitionSpec as P

EPS = 1e-06
TAU = 0.02


def unit_rows(x):
    xf = x.astype(jnp.float32)
    scale = lax.rsqrt(jnp.sum(xf * xf, axis=1, keepdims=True) + EPS)
    return (xf * scale, scale)


def unit_kernel(q_ref, p_ref, q_half, p_half, both, q_scale, p_scale):
    for at, x_ref, half, scale in ((0, p_ref, p_half, p_scale), (1, q_ref, q_half, q_scale)):
        unit, factor = unit_rows(x_ref[...])
        half[...] = unit.astype(jnp.bfloat16)
        both[at] = unit.astype(jnp.bfloat16)
        scale[...] = factor


def unit_halves(queries, passages):
    rows, width = queries.shape
    half = jax.ShapeDtypeStruct((rows, width), jnp.bfloat16)
    scale = jax.ShapeDtypeStruct((rows, 1), jnp.float32)
    return pl.pallas_call(
        unit_kernel,
        out_shape=(half, half, jax.ShapeDtypeStruct((2, rows, width), jnp.bfloat16), scale, scale),
        cost_estimate=pl.CostEstimate(
            flops=8 * rows * width, bytes_accessed=12 * rows * width, transcendentals=0
        ),
        name="unit_halves",
    )(queries, passages)


def pick_kernel(index_ref, pool_ref, out_ref):
    rows = pool_ref.shape[1]
    index = index_ref[0]
    pick = index == lax.broadcasted_iota(jnp.int32, (rows, index.shape[1]), 0)
    found = lax.dot_general(
        pick.astype(jnp.bfloat16),
        pool_ref[0],
        (((0,), (0,)), ((), ())),
        preferred_element_type=jnp.float32,
    )
    out_ref[...] = found.astype(jnp.bfloat16).reshape(out_ref.shape)


def pick_rows(index, pool):
    groups, rows, width = pool.shape
    _, parts, ranks = index.shape
    found = pl.pallas_call(
        pick_kernel,
        grid=(groups,),
        in_specs=[
            pl.BlockSpec((1, 1, parts * ranks), lambda g: (g, 0, 0)),
            pl.BlockSpec((1, rows, width), lambda g: (g, 0, 0)),
        ],
        out_specs=pl.BlockSpec((parts, 1, ranks, width), lambda g: (0, g, 0, 0)),
        out_shape=jax.ShapeDtypeStruct((parts, groups, ranks, width), jnp.bfloat16),
        compiler_params=pltpu.CompilerParams(vmem_limit_bytes=16 * 1024 * 1024),
        cost_estimate=pl.CostEstimate(
            flops=2 * groups * rows * parts * ranks * width,
            bytes_accessed=2 * groups * (rows + parts * ranks) * width,
            transcendentals=0,
        ),
        name="pick_rows",
    )(index.reshape(groups, 1, parts * ranks), pool)
    return found.reshape(parts, groups * ranks, width)


BRIEF = pl.CostEstimate(flops=1000, bytes_accessed=1000, transcendentals=0)
ROOMY = pltpu.CompilerParams(vmem_limit_bytes=32 * 1024 * 1024)
TILE = 256


def exp_kernel(x_ref, own_ref, other_ref, exp_ref, sum_ref):
    half = own_ref.shape[0]
    x = x_ref[...]
    added = jnp.zeros(sum_ref.shape, jnp.float32)
    for at, rows_ref in ((0, own_ref), (half, other_ref)):
        for tile in range(0, half, TILE):
            exps = jnp.exp(dot(x, rows_ref[tile : tile + TILE], 1, 1) / TAU)
            exp_ref[:, at + tile : at + tile + TILE] = exps
            added += jnp.sum(exps, axis=1, keepdims=True)
    sum_ref[...] = added


def exp_scores_of(x, own, other):
    rows = x.shape[0]
    return pl.pallas_call(
        exp_kernel,
        out_shape=(
            jax.ShapeDtypeStruct((rows, 2 * own.shape[0]), jnp.float32),
            jax.ShapeDtypeStruct((rows, 1), jnp.float32),
        ),
        compiler_params=ROOMY,
        cost_estimate=BRIEF,
        name="exp_scores",
    )(x, own, other)


def total_kernel(q_ref, hard_ref, mask_ref, sum_ref, positive_ref, total_ref, w_ref, s_ref, facts_ref):
    rows = q_ref.shape[0]
    q = q_ref[...]
    exps = []
    total = sum_ref[...]
    for tile in range(0, hard_ref.shape[0], TILE):
        scores = dot(q, hard_ref[tile : tile + TILE], 1, 1) / TAU
        exps.append(jnp.where(mask_ref[:, tile : tile + TILE] > 0, jnp.exp(scores), 0.0))
        total += jnp.sum(exps[-1], axis=1, keepdims=True)
    total_ref[...] = total
    for number, exp_hard in enumerate(exps):
        tile = number * TILE
        weights = (exp_hard / total).astype(jnp.bfloat16)
        w_ref[:, tile : tile + TILE] = weights
        s_ref[:, tile : tile + TILE] = jnp.sum(weights.astype(jnp.float32), axis=0, keepdims=True)
    across = lax.broadcasted_iota(jnp.int32, (rows, rows), 0)
    down = lax.broadcasted_iota(jnp.int32, (rows, rows), 1)
    total_row = jnp.sum(jnp.where(across == down, total, 0.0), axis=0, keepdims=True)
    for device in range(facts_ref.shape[0]):
        facts_ref[device, 0:1] = total_row
        facts_ref[device, 1:2] = positive_ref[...].astype(jnp.float32)


def totals_of(q_half, hard_rows, mask, sums, positive, length):
    rows = q_half.shape[0]
    slots = hard_rows.shape[0]
    return pl.pallas_call(
        total_kernel,
        out_shape=(
            jax.ShapeDtypeStruct((rows, 1), jnp.float32),
            jax.ShapeDtypeStruct((rows, slots), jnp.bfloat16),
            jax.ShapeDtypeStruct((1, slots), jnp.float32),
            jax.ShapeDtypeStruct((length, 2, rows), jnp.float32),
        ),
        compiler_params=ROOMY,
        cost_estimate=BRIEF,
        name="totals",
    )(q_half, hard_rows, mask, sums, positive.reshape(1, rows))


def grad_kernel(exp_ref, total_ref, mark_ref, marks_ref, own, other, w_ref, x_ref, scale_ref, *rest):
    *hards, out_ref = rest
    half = own.shape[0]
    width = x_ref.shape[1]
    target = (mark_ref[...] == marks_ref[...]).astype(jnp.float32)
    grads = (exp_ref[...] / total_ref[...] - target).astype(jnp.bfloat16)
    weights = w_ref[...]
    scale = scale_ref[...]
    directions = []
    along = jnp.zeros(scale.shape, jnp.float32)
    for tile in range(0, width, TILE):
        cols = slice(tile, tile + TILE)
        direction = dot(grads[:, :half], own[:, cols], 1, 0) + dot(grads[:, half:], other[:, cols], 1, 0)
        at = 0
        for hard in hards:
            direction += dot(weights[:, at : at + hard.shape[0]], hard[:, cols], 1, 0)
            at += hard.shape[0]
        direction = direction / TAU
        unit = x_ref[:, cols].astype(jnp.float32) * scale
        along += jnp.sum(unit * direction, axis=1, keepdims=True)
        directions.append(direction)
    for number, direction in enumerate(directions):
        cols = slice(number * TILE, (number + 1) * TILE)
        unit = x_ref[:, cols].astype(jnp.float32) * scale
        out_ref[:, cols] = (scale * (direction - unit * along)).astype(jnp.bfloat16)


def grads_of(exps, total, mark, marks, own, other, weights, hard, x, scale):
    return pl.pallas_call(
        grad_kernel,
        out_shape=jax.ShapeDtypeStruct(x.shape, jnp.bfloat16),
        compiler_params=ROOMY,
        cost_estimate=BRIEF,
        name="gradients",
    )(exps, total, mark, marks, own, other, weights, x, scale, *hard)


def dot(a, b, ca, cb):
    return lax.dot_general(a, b, (((ca,), (cb,)), ((), ())), preferred_element_type=jnp.float32)


def exchange(value, axis, groups=None):
    return lax.all_to_all(
        value, axis, split_axis=0, concat_axis=0, tiled=True, axis_index_groups=groups
    )


def shifted(value, axis, move):
    devices = lax.axis_size(axis)
    return lax.ppermute(value, axis, [(i, move(i)) for i in range(devices)])


def beside(i, step, length):
    half = length // 2
    return i // half * half + (i % half // 2 + step) % (half // 2) * 2 + i % 2


def sibling(i):
    return i // 2 * 2 + 1 - i % 2


def blk_order(me):
    length = lax.axis_size("blk")
    where = []
    for core in range(2):
        for step in range(length // 4):
            for z in range(2):
                there = beside((me + length // 2 * z) % length, -step, length)
                where.append(there // 2 * 2 + (there + core) % 2)
    return jnp.stack(where)


def gather_chips(both):
    length = lax.axis_size("blk")

    def turned(value, step):
        return shifted(value, "blk", lambda i: beside(i, step, length))

    over = shifted(both, "blk", lambda i: (i + length // 2) % length)
    pair = jnp.stack([both, over])
    right = turned(pair, 1)
    left = turned(pair, -1)
    far = (turned(right[0], 1), turned(left[1], -1))
    blocks = (both, over, right[0], right[1], far[0], far[1], left[0], left[1])
    return [jnp.concatenate([block[k] for block in blocks]) for k in range(2)]


def local(queries, passages, positive, hard_ids, hard_count):
    rows, width = queries.shape
    hmax = hard_ids.shape[1]
    length = lax.axis_size("blk")
    peers = lax.axis_size("dp")
    me_blk = lax.axis_index("blk")
    me_dp = lax.axis_index("dp")
    nz = 4
    ny = peers // nz
    me_z = me_dp // ny
    me_y = me_dp % ny
    limit = 2 * rows * hmax // peers
    slots = peers * limit
    entries = rows * hmax
    bf16 = jnp.bfloat16

    own_ids = hard_ids.T.reshape(entries)

    q_half, p_half, both, q_scale, p_scale = unit_halves(queries, passages)

    lines = [[z * ny + y for y in range(ny)] for z in range(nz)]
    line_ids = exchange(jnp.broadcast_to(own_ids[None, :], (ny, entries)), "dp", lines)
    q_line = lax.all_gather(q_half, "dp", axis=0, tiled=True, axis_index_groups=lines)

    def along_z(i, step):
        return (i + step * ny) % peers

    p_line = [p_half]
    p_line += [shifted(p_half, "dp", lambda i, t=t: along_z(i, -t)) for t in range(1, nz)]
    p_line = jnp.stack(p_line)

    number = jnp.arange(entries, dtype=jnp.int32)
    ranks = jnp.arange(limit, dtype=jnp.int32)
    turn = jnp.arange(nz, dtype=jnp.int32)
    earlier = (number[:, None] < number[None, :]).astype(bf16)

    coded = (line_ids % rows + 1) * (2 * rows) + (number % rows + 1)[None, :]
    owners = ((me_z + turn) % nz * ny + me_y)[:, None, None]
    mine = line_ids[None] // rows == owners
    count = dot(mine.astype(bf16).reshape(-1, entries), earlier, 1, 0).astype(jnp.int32)
    rank = jnp.where(mine, count.reshape(mine.shape), -1)
    hit = rank[:, :, None, :] == ranks[:, None]
    table = jnp.sum(jnp.where(hit, coded[None, :, None, :], 0), axis=-1)
    asked_row = table // (2 * rows) - 1
    asked_by = table % (2 * rows) - 1

    sent_p = pick_rows(asked_row, p_line)
    got_p = exchange(sent_p, "dp", lines).reshape(slots, width)

    sent_q = pick_rows(jnp.swapaxes(asked_by, 0, 1), q_line.reshape(ny, rows, width))
    got_q = [sent_q[0]]
    got_q += [shifted(sent_q[t], "dp", lambda i, t=t: along_z(i, t)) for t in range(1, nz)]

    p_own, q_own = gather_chips(both)
    p_other = shifted(p_own, "blk", sibling)
    q_other = shifted(q_own, "blk", sibling)
    where = blk_order(me_blk)

    owner = own_ids // rows
    before = (owner[:, None] == owner[None, :]) & (number[None, :] < number[:, None])
    rank = jnp.sum(before.astype(jnp.int32), axis=1)
    step = owner % ny * nz + (owner // ny - me_z) % nz
    place = (step * limit + rank).reshape(hmax, rows)
    used = jnp.arange(hmax, dtype=jnp.int32)[:, None] < hard_count[None, :]
    used_place = jnp.where(used, place, -1)
    slot = jnp.arange(slots, dtype=jnp.int32)
    weighs = jnp.any(used_place[:, :, None] == slot[None, None, :], axis=0)
    wanted = jnp.where(used, own_ids.reshape(hmax, rows) % rows, 0)[:, :, None]
    own_asked = jnp.sum(
        jnp.where(used_place[:, :, None] == slot[None, None, :], wanted, 0), axis=(0, 1)
    )

    exp_scores, sums = exp_scores_of(q_half, p_own, p_other)
    exp_back, _ = exp_scores_of(p_half, q_own, q_other)
    sums, *got_q = lax.optimization_barrier((sums, *got_q))
    total, weights, slot_weights, facts = totals_of(
        q_half, got_p, weighs.astype(jnp.float32), sums, positive, length
    )

    peer = jnp.arange(peers, dtype=jnp.int32)
    step_of = (me_z + peer % nz) % nz * ny + peer // nz
    by_slot = jnp.stack([slot_weights[0], own_asked.astype(jnp.float32)])
    by_slot = by_slot.reshape(2, 1, peers, limit)
    to_owner = peer[:, None] == step_of[None, :]
    by_owner = jnp.sum(jnp.where(to_owner[None, :, :, None], by_slot, 0.0), axis=2)
    got = exchange(jnp.swapaxes(by_owner, 0, 1), "dp")
    from_z = ((me_z - turn) % nz)[:, None] == turn[None, :]
    got = got.reshape(1, nz, ny, 2, limit)
    got = jnp.sum(jnp.where(from_z[:, :, None, None, None], got, 0.0), axis=1)
    got_weights = got[:, :, 0].reshape(1, slots)
    asked = got[:, :, 1].reshape(1, slots).astype(jnp.int32)
    names = asked == jnp.arange(rows, dtype=jnp.int32)[:, None]
    hard_back = jnp.where(names, got_weights, 0.0).astype(bf16)
    facts = exchange(facts, "blk")[where]
    all_total = facts[:, 0].reshape(1, length * rows)
    all_positive = facts[:, 1].reshape(1, length * rows).astype(jnp.int32)

    row = jnp.arange(rows, dtype=jnp.int32)
    column = (where[:, None] * rows + row[None, :]).reshape(1, length * rows)
    own_row = me_blk * rows + row[:, None]
    query_grads = grads_of(
        exp_scores, total, positive[:, None], column,
        p_own, p_other, weights, [got_p], queries, q_scale,
    )
    passage_grads = grads_of(
        exp_back, all_total, own_row, all_positive,
        q_own, q_other, hard_back, got_q, passages, p_scale,
    )
    return (query_grads, passage_grads)


def solution(mesh):
    return jax.shard_map(
        local,
        mesh=mesh,
        in_specs=(
            P(("blk", "dp"), None),
            P(("blk", "dp"), None),
            P(("blk", "dp")),
            P(("blk", "dp"), None),
            P(("blk", "dp")),
        ),
        out_specs=(P(("blk", "dp"), None), P(("blk", "dp"), None)),
        check_vma=False,
    )
```

```python
import jax
import jax.numpy as jnp
from jax import lax
from jax.experimental import pallas as pl
from jax.experimental.pallas import tpu as pltpu
from jax.sharding import PartitionSpec as P

EPS = 1e-06
TAU = 0.02


def unit_rows(x):
    xf = x.astype(jnp.float32)
    scale = lax.rsqrt(jnp.sum(xf * xf, axis=1, keepdims=True) + EPS)
    return (xf * scale, scale)


def unit_kernel(q_ref, p_ref, q_half, p_half, both, q_scale, p_scale):
    for at, x_ref, half, scale in ((0, p_ref, p_half, p_scale), (1, q_ref, q_half, q_scale)):
        unit, factor = unit_rows(x_ref[...])
        half[...] = unit.astype(jnp.bfloat16)
        both[at] = unit.astype(jnp.bfloat16)
        scale[...] = factor


def unit_halves(queries, passages):
    rows, width = queries.shape
    half = jax.ShapeDtypeStruct((rows, width), jnp.bfloat16)
    scale = jax.ShapeDtypeStruct((rows, 1), jnp.float32)
    return pl.pallas_call(
        unit_kernel,
        out_shape=(half, half, jax.ShapeDtypeStruct((2, rows, width), jnp.bfloat16), scale, scale),
        cost_estimate=pl.CostEstimate(
            flops=8 * rows * width, bytes_accessed=12 * rows * width, transcendentals=0
        ),
        name="unit_halves",
    )(queries, passages)


def pick_kernel(index_ref, pool_ref, out_ref):
    rows = pool_ref.shape[1]
    index = index_ref[0]
    pick = index == lax.broadcasted_iota(jnp.int32, (rows, index.shape[1]), 0)
    found = lax.dot_general(
        pick.astype(jnp.bfloat16),
        pool_ref[0],
        (((0,), (0,)), ((), ())),
        preferred_element_type=jnp.float32,
    )
    out_ref[...] = found.astype(jnp.bfloat16).reshape(out_ref.shape)


def pick_rows(index, pool):
    groups, rows, width = pool.shape
    _, parts, ranks = index.shape
    found = pl.pallas_call(
        pick_kernel,
        grid=(groups,),
        in_specs=[
            pl.BlockSpec((1, 1, parts * ranks), lambda g: (g, 0, 0)),
            pl.BlockSpec((1, rows, width), lambda g: (g, 0, 0)),
        ],
        out_specs=pl.BlockSpec((parts, 1, ranks, width), lambda g: (0, g, 0, 0)),
        out_shape=jax.ShapeDtypeStruct((parts, groups, ranks, width), jnp.bfloat16),
        compiler_params=pltpu.CompilerParams(vmem_limit_bytes=16 * 1024 * 1024),
        cost_estimate=pl.CostEstimate(
            flops=2 * groups * rows * parts * ranks * width,
            bytes_accessed=2 * groups * (rows + parts * ranks) * width,
            transcendentals=0,
        ),
        name="pick_rows",
    )(index.reshape(groups, 1, parts * ranks), pool)
    return found.reshape(parts, groups * ranks, width)


ROOMY = pltpu.CompilerParams(vmem_limit_bytes=16 * 1024 * 1024)
TILE = 256


def cost(rows, width, columns, exps=0):
    return pl.CostEstimate(
        flops=2 * rows * width * columns,
        bytes_accessed=2 * (rows + columns) * width + 4 * rows * columns,
        transcendentals=exps,
    )


def exp_kernel(x_ref, own_ref, other_ref, exp_ref, sum_ref):
    half = own_ref.shape[0]
    x = x_ref[...]
    added = jnp.zeros(sum_ref.shape, jnp.float32)
    for at, rows_ref in ((0, own_ref), (half, other_ref)):
        for tile in range(0, half, TILE):
            exps = jnp.exp(dot(x, rows_ref[tile : tile + TILE], 1, 1) / TAU)
            exp_ref[:, at + tile : at + tile + TILE] = exps
            added += jnp.sum(exps, axis=1, keepdims=True)
    sum_ref[...] = added


def exp_scores_of(x, own, other):
    rows = x.shape[0]
    return pl.pallas_call(
        exp_kernel,
        out_shape=(
            jax.ShapeDtypeStruct((rows, 2 * own.shape[0]), jnp.float32),
            jax.ShapeDtypeStruct((rows, 1), jnp.float32),
        ),
        compiler_params=ROOMY,
        cost_estimate=cost(rows, x.shape[1], 2 * own.shape[0], 2 * rows * own.shape[0]),
        name="exp_scores",
    )(x, own, other)


def total_kernel(q_ref, hard_ref, mask_ref, sum_ref, positive_ref, total_ref, w_ref, s_ref, facts_ref):
    rows = q_ref.shape[0]
    q = q_ref[...]
    exps = []
    total = sum_ref[...]
    for tile in range(0, hard_ref.shape[0], TILE):
        scores = dot(q, hard_ref[tile : tile + TILE], 1, 1) / TAU
        exps.append(jnp.where(mask_ref[:, tile : tile + TILE] > 0, jnp.exp(scores), 0.0))
        total += jnp.sum(exps[-1], axis=1, keepdims=True)
    total_ref[...] = total
    for number, exp_hard in enumerate(exps):
        tile = number * TILE
        weights = (exp_hard / total).astype(jnp.bfloat16)
        w_ref[:, tile : tile + TILE] = weights
        s_ref[:, tile : tile + TILE] = jnp.sum(weights.astype(jnp.float32), axis=0, keepdims=True)
    across = lax.broadcasted_iota(jnp.int32, (rows, rows), 0)
    down = lax.broadcasted_iota(jnp.int32, (rows, rows), 1)
    total_row = jnp.sum(jnp.where(across == down, total, 0.0), axis=0, keepdims=True)
    for device in range(facts_ref.shape[0]):
        facts_ref[device, 0:1] = total_row
        facts_ref[device, 1:2] = positive_ref[...].astype(jnp.float32)


def totals_of(q_half, hard_rows, mask, sums, positive, length):
    rows = q_half.shape[0]
    slots = hard_rows.shape[0]
    return pl.pallas_call(
        total_kernel,
        out_shape=(
            jax.ShapeDtypeStruct((rows, 1), jnp.float32),
            jax.ShapeDtypeStruct((rows, slots), jnp.bfloat16),
            jax.ShapeDtypeStruct((1, slots), jnp.float32),
            jax.ShapeDtypeStruct((length, 2, rows), jnp.float32),
        ),
        compiler_params=ROOMY,
        cost_estimate=cost(rows, q_half.shape[1], slots, rows * slots),
        name="totals",
    )(q_half, hard_rows, mask, sums, positive.reshape(1, rows))


def grad_kernel(exp_ref, total_ref, mark_ref, marks_ref, own, other, w_ref, x_ref, scale_ref, *rest):
    *hards, out_ref = rest
    half = own.shape[0]
    width = x_ref.shape[1]
    target = (mark_ref[...] == marks_ref[...]).astype(jnp.float32)
    grads = (exp_ref[...] / total_ref[...] - target).astype(jnp.bfloat16)
    weights = w_ref[...]
    scale = scale_ref[...]
    directions = []
    along = jnp.zeros(scale.shape, jnp.float32)
    for tile in range(0, width, TILE):
        cols = slice(tile, tile + TILE)
        direction = dot(grads[:, :half], own[:, cols], 1, 0) + dot(grads[:, half:], other[:, cols], 1, 0)
        at = 0
        for hard in hards:
            direction += dot(weights[:, at : at + hard.shape[0]], hard[:, cols], 1, 0)
            at += hard.shape[0]
        direction = direction / TAU
        unit = x_ref[:, cols].astype(jnp.float32) * scale
        along += jnp.sum(unit * direction, axis=1, keepdims=True)
        directions.append(direction)
    for number, direction in enumerate(directions):
        cols = slice(number * TILE, (number + 1) * TILE)
        unit = x_ref[:, cols].astype(jnp.float32) * scale
        out_ref[:, cols] = (scale * (direction - unit * along)).astype(jnp.bfloat16)


def grads_of(exps, total, mark, marks, own, other, weights, hard, x, scale):
    return pl.pallas_call(
        grad_kernel,
        out_shape=jax.ShapeDtypeStruct(x.shape, jnp.bfloat16),
        compiler_params=ROOMY,
        cost_estimate=cost(*x.shape, exps.shape[1] + weights.shape[1]),
        name="gradients",
    )(exps, total, mark, marks, own, other, weights, x, scale, *hard)


def dot(a, b, ca, cb):
    return lax.dot_general(a, b, (((ca,), (cb,)), ((), ())), preferred_element_type=jnp.float32)


def exchange(value, axis, groups=None):
    return lax.all_to_all(
        value, axis, split_axis=0, concat_axis=0, tiled=True, axis_index_groups=groups
    )


def shifted(value, axis, move):
    devices = lax.axis_size(axis)
    return lax.ppermute(value, axis, [(i, move(i)) for i in range(devices)])


def beside(i, step, length):
    half = length // 2
    return i // half * half + (i % half // 2 + step) % (half // 2) * 2 + i % 2


def sibling(i):
    return i // 2 * 2 + 1 - i % 2


def blk_order(me):
    length = lax.axis_size("blk")
    where = []
    for core in range(2):
        for step in range(length // 4):
            for z in range(2):
                there = beside((me + length // 2 * z) % length, -step, length)
                where.append(there // 2 * 2 + (there + core) % 2)
    return jnp.stack(where)


def gather_chips(both):
    length = lax.axis_size("blk")

    def turned(value, step):
        return shifted(value, "blk", lambda i: beside(i, step, length))

    over = shifted(both, "blk", lambda i: (i + length // 2) % length)
    pair = jnp.stack([both, over])
    right = turned(pair, 1)
    left = turned(pair, -1)
    far = (turned(right[0], 1), turned(left[1], -1))
    blocks = (both, over, right[0], right[1], far[0], far[1], left[0], left[1])
    return [jnp.concatenate([block[k] for block in blocks]) for k in range(2)]


def local(queries, passages, positive, hard_ids, hard_count):
    rows, width = queries.shape
    hmax = hard_ids.shape[1]
    length = lax.axis_size("blk")
    peers = lax.axis_size("dp")
    me_blk = lax.axis_index("blk")
    me_dp = lax.axis_index("dp")
    nz = 4
    ny = peers // nz
    me_z = me_dp // ny
    me_y = me_dp % ny
    limit = 2 * rows * hmax // peers
    slots = peers * limit
    entries = rows * hmax
    bf16 = jnp.bfloat16

    own_ids = hard_ids.T.reshape(entries)

    q_half, p_half, both, q_scale, p_scale = unit_halves(queries, passages)

    lines = [[z * ny + y for y in range(ny)] for z in range(nz)]
    line_ids = exchange(jnp.broadcast_to(own_ids[None, :], (ny, entries)), "dp", lines)
    q_line = lax.all_gather(q_half, "dp", axis=0, tiled=True, axis_index_groups=lines)

    def along_z(i, step):
        return (i + step * ny) % peers

    p_line = [p_half]
    p_line += [shifted(p_half, "dp", lambda i, t=t: along_z(i, -t)) for t in range(1, nz)]
    p_line = jnp.stack(p_line)

    number = jnp.arange(entries, dtype=jnp.int32)
    ranks = jnp.arange(limit, dtype=jnp.int32)
    turn = jnp.arange(nz, dtype=jnp.int32)
    earlier = (number[:, None] < number[None, :]).astype(bf16)

    coded = (line_ids % rows + 1) * (2 * rows) + (number % rows + 1)[None, :]
    owners = ((me_z + turn) % nz * ny + me_y)[:, None, None]
    mine = line_ids[None] // rows == owners
    count = dot(mine.astype(bf16).reshape(-1, entries), earlier, 1, 0).astype(jnp.int32)
    rank = jnp.where(mine, count.reshape(mine.shape), -1)
    hit = rank[:, :, None, :] == ranks[:, None]
    table = jnp.sum(jnp.where(hit, coded[None, :, None, :], 0), axis=-1)
    asked_row = table // (2 * rows) - 1
    asked_by = table % (2 * rows) - 1

    sent_p = pick_rows(asked_row, p_line)
    got_p = exchange(sent_p, "dp", lines).reshape(slots, width)

    sent_q = pick_rows(jnp.swapaxes(asked_by, 0, 1), q_line.reshape(ny, rows, width))
    got_q = [sent_q[0]]
    got_q += [shifted(sent_q[t], "dp", lambda i, t=t: along_z(i, t)) for t in range(1, nz)]

    p_own, q_own = gather_chips(both)
    p_own, got_q[1] = lax.optimization_barrier((p_own, got_q[1]))
    q_own, got_q[2], got_q[3] = lax.optimization_barrier((q_own, got_q[2], got_q[3]))
    p_other = shifted(p_own, "blk", sibling)
    q_other = shifted(q_own, "blk", sibling)
    where = blk_order(me_blk)

    owner = own_ids // rows
    before = (owner[:, None] == owner[None, :]) & (number[None, :] < number[:, None])
    rank = jnp.sum(before.astype(jnp.int32), axis=1)
    step = owner % ny * nz + (owner // ny - me_z) % nz
    place = (step * limit + rank).reshape(hmax, rows)
    used = jnp.arange(hmax, dtype=jnp.int32)[:, None] < hard_count[None, :]
    used_place = jnp.where(used, place, -1)
    slot = jnp.arange(slots, dtype=jnp.int32)
    weighs = jnp.any(used_place[:, :, None] == slot[None, None, :], axis=0)
    wanted = jnp.where(used, own_ids.reshape(hmax, rows) % rows, 0)[:, :, None]
    own_asked = jnp.sum(
        jnp.where(used_place[:, :, None] == slot[None, None, :], wanted, 0), axis=(0, 1)
    )

    exp_scores, sums = exp_scores_of(q_half, p_own, p_other)
    sums, q_other = lax.optimization_barrier((sums, q_other))
    exp_back, _ = exp_scores_of(p_half, q_own, q_other)
    total, weights, slot_weights, facts = totals_of(
        q_half, got_p, weighs.astype(jnp.float32), sums, positive, length
    )

    peer = jnp.arange(peers, dtype=jnp.int32)
    step_of = (me_z + peer % nz) % nz * ny + peer // nz
    by_slot = jnp.stack([slot_weights[0], own_asked.astype(jnp.float32)])
    by_slot = by_slot.reshape(2, 1, peers, limit)
    to_owner = peer[:, None] == step_of[None, :]
    by_owner = jnp.sum(jnp.where(to_owner[None, :, :, None], by_slot, 0.0), axis=2)
    facts = exchange(facts, "blk")
    facts, by_owner, exp_scores, total = lax.optimization_barrier(
        (facts, by_owner, exp_scores, total)
    )
    got = exchange(jnp.swapaxes(by_owner, 0, 1), "dp")
    from_z = ((me_z - turn) % nz)[:, None] == turn[None, :]
    got = got.reshape(1, nz, ny, 2, limit)
    got = jnp.sum(jnp.where(from_z[:, :, None, None, None], got, 0.0), axis=1)
    got_weights = got[:, :, 0].reshape(1, slots)
    asked = got[:, :, 1].reshape(1, slots).astype(jnp.int32)
    names = asked == jnp.arange(rows, dtype=jnp.int32)[:, None]
    hard_back = jnp.where(names, got_weights, 0.0).astype(bf16)
    facts = facts[where]
    all_total = facts[:, 0].reshape(1, length * rows)
    all_positive = facts[:, 1].reshape(1, length * rows).astype(jnp.int32)

    row = jnp.arange(rows, dtype=jnp.int32)
    column = (where[:, None] * rows + row[None, :]).reshape(1, length * rows)
    own_row = me_blk * rows + row[:, None]
    query_grads = grads_of(
        exp_scores, total, positive[:, None], column,
        p_own, p_other, weights, [got_p], queries, q_scale,
    )
    passage_grads = grads_of(
        exp_back, all_total, own_row, all_positive,
        q_own, q_other, hard_back, got_q, passages, p_scale,
    )
    return (query_grads, passage_grads)


def solution(mesh):
    return jax.shard_map(
        local,
        mesh=mesh,
        in_specs=(
            P(("blk", "dp"), None),
            P(("blk", "dp"), None),
            P(("blk", "dp")),
            P(("blk", "dp"), None),
            P(("blk", "dp")),
        ),
        out_specs=(P(("blk", "dp"), None), P(("blk", "dp"), None)),
        check_vma=False,
    )
```

```python
import jax
import jax.numpy as jnp
from jax import lax
from jax.experimental import pallas as pl
from jax.experimental.pallas import tpu as pltpu
from jax.sharding import PartitionSpec as P

EPS = 1e-06
TAU = 0.02


def unit_rows(x):
    xf = x.astype(jnp.float32)
    scale = lax.rsqrt(jnp.sum(xf * xf, axis=1, keepdims=True) + EPS)
    return (xf * scale, scale)


def unit_kernel(q_ref, p_ref, q_half, p_half, both, q_scale, p_scale):
    for at, x_ref, half, scale in ((0, p_ref, p_half, p_scale), (1, q_ref, q_half, q_scale)):
        unit, factor = unit_rows(x_ref[...])
        half[...] = unit.astype(jnp.bfloat16)
        both[at] = unit.astype(jnp.bfloat16)
        scale[...] = factor


def unit_halves(queries, passages):
    rows, width = queries.shape
    half = jax.ShapeDtypeStruct((rows, width), jnp.bfloat16)
    scale = jax.ShapeDtypeStruct((rows, 1), jnp.float32)
    return pl.pallas_call(
        unit_kernel,
        out_shape=(half, half, jax.ShapeDtypeStruct((2, rows, width), jnp.bfloat16), scale, scale),
        cost_estimate=pl.CostEstimate(
            flops=8 * rows * width, bytes_accessed=12 * rows * width, transcendentals=0
        ),
        name="unit_halves",
    )(queries, passages)


def pick_kernel(index_ref, pool_ref, out_ref):
    rows = pool_ref.shape[1]
    index = index_ref[0]
    pick = index == lax.broadcasted_iota(jnp.int32, (rows, index.shape[1]), 0)
    found = lax.dot_general(
        pick.astype(jnp.bfloat16),
        pool_ref[0],
        (((0,), (0,)), ((), ())),
        preferred_element_type=jnp.float32,
    )
    out_ref[...] = found.astype(jnp.bfloat16).reshape(out_ref.shape)


def pick_rows(index, pool):
    groups, rows, width = pool.shape
    _, parts, ranks = index.shape
    found = pl.pallas_call(
        pick_kernel,
        grid=(groups,),
        in_specs=[
            pl.BlockSpec((1, 1, parts * ranks), lambda g: (g, 0, 0)),
            pl.BlockSpec((1, rows, width), lambda g: (g, 0, 0)),
        ],
        out_specs=pl.BlockSpec((parts, 1, ranks, width), lambda g: (0, g, 0, 0)),
        out_shape=jax.ShapeDtypeStruct((parts, groups, ranks, width), jnp.bfloat16),
        compiler_params=room(4),
        cost_estimate=pl.CostEstimate(
            flops=2 * groups * rows * parts * ranks * width,
            bytes_accessed=2 * groups * (rows + parts * ranks) * width,
            transcendentals=0,
        ),
        name="pick_rows",
    )(index.reshape(groups, 1, parts * ranks), pool)
    return found.reshape(parts, groups * ranks, width)


TILE = 256


def room(mib):
    return pltpu.CompilerParams(vmem_limit_bytes=mib * 1024 * 1024)


def cost(rows, width, columns, exps=0):
    return pl.CostEstimate(
        flops=2 * rows * width * columns,
        bytes_accessed=2 * (rows + columns) * width + 4 * rows * columns,
        transcendentals=exps,
    )


def exp_kernel(x_ref, own_ref, other_ref, exp_ref, sum_ref):
    half = own_ref.shape[0]
    x = x_ref[...]
    added = jnp.zeros(sum_ref.shape, jnp.float32)
    for at, rows_ref in ((0, own_ref), (half, other_ref)):
        for tile in range(0, half, TILE):
            exps = jnp.exp(dot(x, rows_ref[tile : tile + TILE], 1, 1) / TAU)
            exp_ref[:, at + tile : at + tile + TILE] = exps
            added += jnp.sum(exps, axis=1, keepdims=True)
    sum_ref[...] = added


def exp_scores_of(x, own, other):
    rows = x.shape[0]
    return pl.pallas_call(
        exp_kernel,
        out_shape=(
            jax.ShapeDtypeStruct((rows, 2 * own.shape[0]), jnp.float32),
            jax.ShapeDtypeStruct((rows, 1), jnp.float32),
        ),
        compiler_params=room(8),
        cost_estimate=cost(rows, x.shape[1], 2 * own.shape[0], 2 * rows * own.shape[0]),
        name="exp_scores",
    )(x, own, other)


def total_kernel(q_ref, hard_ref, mask_ref, sum_ref, positive_ref, total_ref, w_ref, s_ref, facts_ref):
    rows = q_ref.shape[0]
    q = q_ref[...]
    exps = []
    total = sum_ref[...]
    for tile in range(0, hard_ref.shape[0], TILE):
        scores = dot(q, hard_ref[tile : tile + TILE], 1, 1) / TAU
        exps.append(jnp.where(mask_ref[:, tile : tile + TILE] > 0, jnp.exp(scores), 0.0))
        total += jnp.sum(exps[-1], axis=1, keepdims=True)
    total_ref[...] = total
    for number, exp_hard in enumerate(exps):
        tile = number * TILE
        weights = (exp_hard / total).astype(jnp.bfloat16)
        w_ref[:, tile : tile + TILE] = weights
        s_ref[:, tile : tile + TILE] = jnp.sum(weights.astype(jnp.float32), axis=0, keepdims=True)
    across = lax.broadcasted_iota(jnp.int32, (rows, rows), 0)
    down = lax.broadcasted_iota(jnp.int32, (rows, rows), 1)
    total_row = jnp.sum(jnp.where(across == down, total, 0.0), axis=0, keepdims=True)
    for device in range(facts_ref.shape[0]):
        facts_ref[device, 0:1] = total_row
        facts_ref[device, 1:2] = positive_ref[...].astype(jnp.float32)


def totals_of(q_half, hard_rows, mask, sums, positive, length):
    rows = q_half.shape[0]
    slots = hard_rows.shape[0]
    return pl.pallas_call(
        total_kernel,
        out_shape=(
            jax.ShapeDtypeStruct((rows, 1), jnp.float32),
            jax.ShapeDtypeStruct((rows, slots), jnp.bfloat16),
            jax.ShapeDtypeStruct((1, slots), jnp.float32),
            jax.ShapeDtypeStruct((length, 2, rows), jnp.float32),
        ),
        compiler_params=room(8),
        cost_estimate=cost(rows, q_half.shape[1], slots, rows * slots),
        name="totals",
    )(q_half, hard_rows, mask, sums, positive.reshape(1, rows))


def grad_kernel(exp_ref, total_ref, mark_ref, marks_ref, own, other, w_ref, x_ref, scale_ref, *rest):
    *chunks, out_ref, hard, sems = rest
    copies = []
    at = 0
    for number, chunk in enumerate(chunks):
        place = hard.at[pl.ds(at, chunk.shape[0])]
        copies.append(pltpu.make_async_copy(chunk, place, sems.at[number]))
        copies[-1].start()
        at += chunk.shape[0]
    half = own.shape[0]
    width = x_ref.shape[1]
    target = (mark_ref[...] == marks_ref[...]).astype(jnp.float32)
    grads = (exp_ref[...] / total_ref[...] - target).astype(jnp.bfloat16)
    weights = w_ref[...]
    scale = scale_ref[...]
    directions = []
    for tile in range(0, width, TILE):
        cols = slice(tile, tile + TILE)
        direction = dot(grads[:, :half], own[:, cols], 1, 0)
        directions.append(direction + dot(grads[:, half:], other[:, cols], 1, 0))
    for copy in copies:
        copy.wait()
    along = jnp.zeros(scale.shape, jnp.float32)
    for number in range(len(directions)):
        cols = slice(number * TILE, (number + 1) * TILE)
        direction = (directions[number] + dot(weights, hard[:, cols], 1, 0)) / TAU
        unit = x_ref[:, cols].astype(jnp.float32) * scale
        along += jnp.sum(unit * direction, axis=1, keepdims=True)
        directions[number] = direction
    for number, direction in enumerate(directions):
        cols = slice(number * TILE, (number + 1) * TILE)
        unit = x_ref[:, cols].astype(jnp.float32) * scale
        out_ref[:, cols] = (scale * (direction - unit * along)).astype(jnp.bfloat16)


def grads_of(exps, total, mark, marks, own, other, weights, hard, x, scale):
    operands = (exps, total, mark, marks, own, other, weights, x, scale)
    whole = pl.BlockSpec(memory_space=pltpu.VMEM)
    return pl.pallas_call(
        grad_kernel,
        in_specs=[whole] * len(operands) + [pl.BlockSpec(memory_space=pl.ANY)] * len(hard),
        out_specs=whole,
        out_shape=jax.ShapeDtypeStruct(x.shape, jnp.bfloat16),
        scratch_shapes=[
            pltpu.VMEM((weights.shape[1], x.shape[1]), jnp.bfloat16),
            pltpu.SemaphoreType.DMA((len(hard),)),
        ],
        compiler_params=room(12),
        cost_estimate=cost(*x.shape, exps.shape[1] + weights.shape[1]),
        name="gradients",
    )(*operands, *hard)


def dot(a, b, ca, cb):
    return lax.dot_general(a, b, (((ca,), (cb,)), ((), ())), preferred_element_type=jnp.float32)


def exchange(value, axis, groups=None):
    return lax.all_to_all(
        value, axis, split_axis=0, concat_axis=0, tiled=True, axis_index_groups=groups
    )


def shifted(value, axis, move):
    devices = lax.axis_size(axis)
    return lax.ppermute(value, axis, [(i, move(i)) for i in range(devices)])


def beside(i, step, length):
    half = length // 2
    return i // half * half + (i % half // 2 + step) % (half // 2) * 2 + i % 2


def sibling(i):
    return i // 2 * 2 + 1 - i % 2


def blk_order(me):
    length = lax.axis_size("blk")
    where = []
    for core in range(2):
        for step in range(length // 4):
            for z in range(2):
                there = beside((me + length // 2 * z) % length, -step, length)
                where.append(there // 2 * 2 + (there + core) % 2)
    return jnp.stack(where)


def gather_chips(both, after):
    length = lax.axis_size("blk")

    def turned(value, step):
        return shifted(value, "blk", lambda i: beside(i, step, length))

    over = shifted(both, "blk", lambda i: (i + length // 2) % length)
    over, after = lax.optimization_barrier((over, after))
    pair = jnp.stack([both, over])
    right = turned(pair, 1)
    left = turned(pair, -1)
    far = (turned(right[0], 1), turned(left[1], -1))
    blocks = (both, over, right[0], right[1], far[0], far[1], left[0], left[1])
    return [jnp.concatenate([block[k] for block in blocks]) for k in range(2)], after


def local(queries, passages, positive, hard_ids, hard_count):
    rows, width = queries.shape
    hmax = hard_ids.shape[1]
    length = lax.axis_size("blk")
    peers = lax.axis_size("dp")
    me_blk = lax.axis_index("blk")
    me_dp = lax.axis_index("dp")
    nz = 4
    ny = peers // nz
    me_z = me_dp // ny
    me_y = me_dp % ny
    limit = 2 * rows * hmax // peers
    slots = peers * limit
    entries = rows * hmax
    bf16 = jnp.bfloat16

    own_ids = hard_ids.T.reshape(entries)

    q_half, p_half, both, q_scale, p_scale = unit_halves(queries, passages)

    lines = [[z * ny + y for y in range(ny)] for z in range(nz)]
    line_ids = exchange(jnp.broadcast_to(own_ids[None, :], (ny, entries)), "dp", lines)
    q_line = lax.all_gather(q_half, "dp", axis=0, tiled=True, axis_index_groups=lines)

    def along_z(i, step):
        return (i + step * ny) % peers

    p_line = [p_half]
    p_line += [shifted(p_half, "dp", lambda i, t=t: along_z(i, -t)) for t in range(1, nz)]
    p_line = jnp.stack(p_line)

    number = jnp.arange(entries, dtype=jnp.int32)
    ranks = jnp.arange(limit, dtype=jnp.int32)
    turn = jnp.arange(nz, dtype=jnp.int32)
    earlier = (number[:, None] < number[None, :]).astype(bf16)

    coded = (line_ids % rows + 1) * (2 * rows) + (number % rows + 1)[None, :]
    owners = ((me_z + turn) % nz * ny + me_y)[:, None, None]
    mine = line_ids[None] // rows == owners
    count = dot(mine.astype(bf16).reshape(-1, entries), earlier, 1, 0).astype(jnp.int32)
    rank = jnp.where(mine, count.reshape(mine.shape), -1)
    hit = rank[:, :, None, :] == ranks[:, None]
    table = jnp.sum(jnp.where(hit, coded[None, :, None, :], 0), axis=-1)
    asked_row = table // (2 * rows) - 1
    asked_by = table % (2 * rows) - 1

    sent_p = pick_rows(asked_row, p_line)
    got_p = exchange(sent_p, "dp", lines).reshape(slots, width)

    sent_q = pick_rows(jnp.swapaxes(asked_by, 0, 1), q_line.reshape(ny, rows, width))
    (p_own, q_own), sent_q = gather_chips(both, sent_q)
    got_q = [sent_q[0]]
    got_q += [shifted(sent_q[t], "dp", lambda i, t=t: along_z(i, t)) for t in range(1, nz)]

    p_own, got_q[1] = lax.optimization_barrier((p_own, got_q[1]))
    q_own, got_q[2], got_q[3] = lax.optimization_barrier((q_own, got_q[2], got_q[3]))
    p_other = shifted(p_own, "blk", sibling)
    q_other = shifted(q_own, "blk", sibling)
    where = blk_order(me_blk)

    owner = own_ids // rows
    before = (owner[:, None] == owner[None, :]) & (number[None, :] < number[:, None])
    rank = jnp.sum(before.astype(jnp.int32), axis=1)
    step = owner % ny * nz + (owner // ny - me_z) % nz
    place = (step * limit + rank).reshape(hmax, rows)
    used = jnp.arange(hmax, dtype=jnp.int32)[:, None] < hard_count[None, :]
    used_place = jnp.where(used, place, -1)
    slot = jnp.arange(slots, dtype=jnp.int32)
    weighs = jnp.any(used_place[:, :, None] == slot[None, None, :], axis=0)
    wanted = jnp.where(used, own_ids.reshape(hmax, rows) % rows, 0)[:, :, None]
    own_asked = jnp.sum(
        jnp.where(used_place[:, :, None] == slot[None, None, :], wanted, 0), axis=(0, 1)
    )

    exp_scores, sums = exp_scores_of(q_half, p_own, p_other)
    sums, q_other = lax.optimization_barrier((sums, q_other))
    exp_back, _ = exp_scores_of(p_half, q_own, q_other)
    total, weights, slot_weights, facts = totals_of(
        q_half, got_p, weighs.astype(jnp.float32), sums, positive, length
    )

    peer = jnp.arange(peers, dtype=jnp.int32)
    step_of = (me_z + peer % nz) % nz * ny + peer // nz
    by_slot = jnp.stack([slot_weights[0], own_asked.astype(jnp.float32)])
    by_slot = by_slot.reshape(2, 1, peers, limit)
    to_owner = peer[:, None] == step_of[None, :]
    by_owner = jnp.sum(jnp.where(to_owner[None, :, :, None], by_slot, 0.0), axis=2)
    facts = exchange(facts, "blk")
    facts, by_owner, exp_scores, total = lax.optimization_barrier(
        (facts, by_owner, exp_scores, total)
    )
    got = exchange(jnp.swapaxes(by_owner, 0, 1), "dp")
    from_z = ((me_z - turn) % nz)[:, None] == turn[None, :]
    got = got.reshape(1, nz, ny, 2, limit)
    got = jnp.sum(jnp.where(from_z[:, :, None, None, None], got, 0.0), axis=1)
    got_weights = got[:, :, 0].reshape(1, slots)
    asked = got[:, :, 1].reshape(1, slots).astype(jnp.int32)
    names = asked == jnp.arange(rows, dtype=jnp.int32)[:, None]
    hard_back = jnp.where(names, got_weights, 0.0).astype(bf16)
    facts = facts[where]
    all_total = facts[:, 0].reshape(1, length * rows)
    all_positive = facts[:, 1].reshape(1, length * rows).astype(jnp.int32)

    row = jnp.arange(rows, dtype=jnp.int32)
    column = (where[:, None] * rows + row[None, :]).reshape(1, length * rows)
    own_row = me_blk * rows + row[:, None]
    query_grads = grads_of(
        exp_scores, total, positive[:, None], column,
        p_own, p_other, weights, [got_p], queries, q_scale,
    )
    passage_grads = grads_of(
        exp_back, all_total, own_row, all_positive,
        q_own, q_other, hard_back, got_q, passages, p_scale,
    )
    return (query_grads, passage_grads)


def solution(mesh):
    return jax.shard_map(
        local,
        mesh=mesh,
        in_specs=(
            P(("blk", "dp"), None),
            P(("blk", "dp"), None),
            P(("blk", "dp")),
            P(("blk", "dp"), None),
            P(("blk", "dp")),
        ),
        out_specs=(P(("blk", "dp"), None), P(("blk", "dp"), None)),
        check_vma=False,
    )
```

```python
import jax
import jax.numpy as jnp
from jax import lax
from jax.experimental import pallas as pl
from jax.experimental.pallas import tpu as pltpu
from jax.sharding import PartitionSpec as P

EPS = 1e-06
TAU = 0.02
ROOMY = pltpu.CompilerParams(vmem_limit_bytes=56 * 1024 * 1024)


def unit_rows(x):
    xf = x.astype(jnp.float32)
    scale = lax.rsqrt(jnp.sum(xf * xf, axis=1, keepdims=True) + EPS)
    return (xf * scale, scale)


def unit_kernel(q_ref, p_ref, q_half, p_half, both, q_scale, p_scale):
    for at, x_ref, half, scale in ((0, p_ref, p_half, p_scale), (1, q_ref, q_half, q_scale)):
        unit, factor = unit_rows(x_ref[...])
        half[...] = unit.astype(jnp.bfloat16)
        both[at] = unit.astype(jnp.bfloat16)
        scale[...] = factor


def unit_halves(queries, passages):
    rows, width = queries.shape
    half = jax.ShapeDtypeStruct((rows, width), jnp.bfloat16)
    scale = jax.ShapeDtypeStruct((rows, 1), jnp.float32)
    return pl.pallas_call(
        unit_kernel,
        out_shape=(half, half, jax.ShapeDtypeStruct((2, rows, width), jnp.bfloat16), scale, scale),
        cost_estimate=pl.CostEstimate(
            flops=8 * rows * width, bytes_accessed=12 * rows * width, transcendentals=0
        ),
        name="unit_halves",
    )(queries, passages)


def pick_kernel(index_ref, pool_ref, out_ref):
    rows = pool_ref.shape[1]
    index = index_ref[0]
    pick = index == lax.broadcasted_iota(jnp.int32, (rows, index.shape[1]), 0)
    found = lax.dot_general(
        pick.astype(jnp.bfloat16),
        pool_ref[0],
        (((0,), (0,)), ((), ())),
        preferred_element_type=jnp.float32,
    )
    out_ref[...] = found.astype(jnp.bfloat16).reshape(out_ref.shape)


def pick_rows(index, pool):
    groups, rows, width = pool.shape
    _, parts, ranks = index.shape
    found = pl.pallas_call(
        pick_kernel,
        grid=(groups,),
        in_specs=[
            pl.BlockSpec((1, 1, parts * ranks), lambda g: (g, 0, 0)),
            pl.BlockSpec((1, rows, width), lambda g: (g, 0, 0)),
        ],
        out_specs=pl.BlockSpec((parts, 1, ranks, width), lambda g: (0, g, 0, 0)),
        out_shape=jax.ShapeDtypeStruct((parts, groups, ranks, width), jnp.bfloat16),
        compiler_params=ROOMY,
        cost_estimate=pl.CostEstimate(
            flops=2 * groups * rows * parts * ranks * width,
            bytes_accessed=2 * groups * (rows + parts * ranks) * width,
            transcendentals=0,
        ),
        name="pick_rows",
    )(index.reshape(groups, 1, parts * ranks), pool)
    return found.reshape(parts, groups * ranks, width)


TILE = 256


def cost(rows, width, columns, exps=0):
    return pl.CostEstimate(
        flops=2 * rows * width * columns,
        bytes_accessed=2 * (rows + columns) * width + 4 * rows * columns,
        transcendentals=exps,
    )


def exp_kernel(x_ref, own_ref, other_ref, exp_ref, sum_ref):
    half = own_ref.shape[0]
    x = x_ref[...]
    added = jnp.zeros(sum_ref.shape, jnp.float32)
    for at, rows_ref in ((0, own_ref), (half, other_ref)):
        for tile in range(0, half, TILE):
            exps = jnp.exp(dot(x, rows_ref[tile : tile + TILE], 1, 1) / TAU)
            exp_ref[:, at + tile : at + tile + TILE] = exps
            added += jnp.sum(exps, axis=1, keepdims=True)
    sum_ref[...] = added


def exp_scores_of(x, own, other):
    rows = x.shape[0]
    return pl.pallas_call(
        exp_kernel,
        out_shape=(
            jax.ShapeDtypeStruct((rows, 2 * own.shape[0]), jnp.float32),
            jax.ShapeDtypeStruct((rows, 1), jnp.float32),
        ),
        compiler_params=ROOMY,
        cost_estimate=cost(rows, x.shape[1], 2 * own.shape[0], 2 * rows * own.shape[0]),
        name="exp_scores",
    )(x, own, other)


def total_kernel(q_ref, hard_ref, mask_ref, sum_ref, positive_ref, total_ref, w_ref, s_ref, facts_ref):
    rows = q_ref.shape[0]
    q = q_ref[...]
    exps = []
    total = sum_ref[...]
    for tile in range(0, hard_ref.shape[0], TILE):
        scores = dot(q, hard_ref[tile : tile + TILE], 1, 1) / TAU
        exps.append(jnp.where(mask_ref[:, tile : tile + TILE] > 0, jnp.exp(scores), 0.0))
        total += jnp.sum(exps[-1], axis=1, keepdims=True)
    total_ref[...] = total
    for number, exp_hard in enumerate(exps):
        tile = number * TILE
        weights = (exp_hard / total).astype(jnp.bfloat16)
        w_ref[:, tile : tile + TILE] = weights
        s_ref[:, tile : tile + TILE] = jnp.sum(weights.astype(jnp.float32), axis=0, keepdims=True)
    across = lax.broadcasted_iota(jnp.int32, (rows, rows), 0)
    down = lax.broadcasted_iota(jnp.int32, (rows, rows), 1)
    total_row = jnp.sum(jnp.where(across == down, total, 0.0), axis=0, keepdims=True)
    for device in range(facts_ref.shape[0]):
        facts_ref[device, 0:1] = total_row
        facts_ref[device, 1:2] = positive_ref[...].astype(jnp.float32)


def totals_of(q_half, hard_rows, mask, sums, positive, length):
    rows = q_half.shape[0]
    slots = hard_rows.shape[0]
    return pl.pallas_call(
        total_kernel,
        out_shape=(
            jax.ShapeDtypeStruct((rows, 1), jnp.float32),
            jax.ShapeDtypeStruct((rows, slots), jnp.bfloat16),
            jax.ShapeDtypeStruct((1, slots), jnp.float32),
            jax.ShapeDtypeStruct((length, 2, rows), jnp.float32),
        ),
        compiler_params=ROOMY,
        cost_estimate=cost(rows, q_half.shape[1], slots, rows * slots),
        name="totals",
    )(q_half, hard_rows, mask, sums, positive.reshape(1, rows))


def grad_kernel(exp_ref, total_ref, mark_ref, marks_ref, own, other, w_ref, x_ref, scale_ref, *rest):
    *chunks, out_ref, hard, sems = rest
    copies = []
    at = 0
    for number, chunk in enumerate(chunks):
        place = hard.at[pl.ds(at, chunk.shape[0])]
        copies.append(pltpu.make_async_copy(chunk, place, sems.at[number]))
        copies[-1].start()
        at += chunk.shape[0]
    half = own.shape[0]
    width = x_ref.shape[1]
    target = (mark_ref[...] == marks_ref[...]).astype(jnp.float32)
    grads = (exp_ref[...] / total_ref[...] - target).astype(jnp.bfloat16)
    weights = w_ref[...]
    scale = scale_ref[...]
    directions = []
    for tile in range(0, width, TILE):
        cols = slice(tile, tile + TILE)
        direction = dot(grads[:, :half], own[:, cols], 1, 0)
        directions.append(direction + dot(grads[:, half:], other[:, cols], 1, 0))
    for copy in copies:
        copy.wait()
    along = jnp.zeros(scale.shape, jnp.float32)
    for number in range(len(directions)):
        cols = slice(number * TILE, (number + 1) * TILE)
        direction = (directions[number] + dot(weights, hard[:, cols], 1, 0)) / TAU
        unit = x_ref[:, cols].astype(jnp.float32) * scale
        along += jnp.sum(unit * direction, axis=1, keepdims=True)
        directions[number] = direction
    for number, direction in enumerate(directions):
        cols = slice(number * TILE, (number + 1) * TILE)
        unit = x_ref[:, cols].astype(jnp.float32) * scale
        out_ref[:, cols] = (scale * (direction - unit * along)).astype(jnp.bfloat16)


def grads_of(exps, total, mark, marks, own, other, weights, hard, x, scale):
    operands = (exps, total, mark, marks, own, other, weights, x, scale)
    whole = pl.BlockSpec(memory_space=pltpu.VMEM)
    return pl.pallas_call(
        grad_kernel,
        in_specs=[whole] * len(operands) + [pl.BlockSpec(memory_space=pl.ANY)] * len(hard),
        out_specs=whole,
        out_shape=jax.ShapeDtypeStruct(x.shape, jnp.bfloat16),
        scratch_shapes=[
            pltpu.VMEM((weights.shape[1], x.shape[1]), jnp.bfloat16),
            pltpu.SemaphoreType.DMA((len(hard),)),
        ],
        compiler_params=ROOMY,
        cost_estimate=cost(*x.shape, exps.shape[1] + weights.shape[1]),
        name="gradients",
    )(*operands, *hard)


def dot(a, b, ca, cb):
    return lax.dot_general(a, b, (((ca,), (cb,)), ((), ())), preferred_element_type=jnp.float32)


def exchange(value, axis, groups=None):
    return lax.all_to_all(
        value, axis, split_axis=0, concat_axis=0, tiled=True, axis_index_groups=groups
    )


def shifted(value, axis, move):
    devices = lax.axis_size(axis)
    return lax.ppermute(value, axis, [(i, move(i)) for i in range(devices)])


def beside(i, step, length):
    half = length // 2
    return i // half * half + (i % half // 2 + step) % (half // 2) * 2 + i % 2


def sibling(i):
    return i // 2 * 2 + 1 - i % 2


def blk_order(me):
    length = lax.axis_size("blk")
    where = []
    for core in range(2):
        for step in range(length // 4):
            for z in range(2):
                there = beside((me + length // 2 * z) % length, -step, length)
                where.append(there // 2 * 2 + (there + core) % 2)
    return jnp.stack(where)


def gather_chips(both, after):
    length = lax.axis_size("blk")

    def turned(value, step):
        return shifted(value, "blk", lambda i: beside(i, step, length))

    over = shifted(both, "blk", lambda i: (i + length // 2) % length)
    over, after = lax.optimization_barrier((over, after))
    pair = jnp.stack([both, over])
    right = turned(pair, 1)
    left = turned(pair, -1)
    far = (turned(right[0], 1), turned(left[1], -1))
    blocks = (both, over, right[0], right[1], far[0], far[1], left[0], left[1])
    return [jnp.concatenate([block[k] for block in blocks]) for k in range(2)], after


def local(queries, passages, positive, hard_ids, hard_count):
    rows, width = queries.shape
    hmax = hard_ids.shape[1]
    length = lax.axis_size("blk")
    peers = lax.axis_size("dp")
    me_blk = lax.axis_index("blk")
    me_dp = lax.axis_index("dp")
    nz = 4
    ny = peers // nz
    me_z = me_dp // ny
    me_y = me_dp % ny
    limit = 2 * rows * hmax // peers
    slots = peers * limit
    entries = rows * hmax
    bf16 = jnp.bfloat16

    own_ids = hard_ids.T.reshape(entries)

    q_half, p_half, both, q_scale, p_scale = unit_halves(queries, passages)

    lines = [[z * ny + y for y in range(ny)] for z in range(nz)]
    line_ids = exchange(jnp.broadcast_to(own_ids[None, :], (ny, entries)), "dp", lines)
    q_line = lax.all_gather(q_half, "dp", axis=0, tiled=True, axis_index_groups=lines)

    def along_z(i, step):
        return (i + step * ny) % peers

    p_line = [p_half]
    p_line += [shifted(p_half, "dp", lambda i, t=t: along_z(i, -t)) for t in range(1, nz)]
    p_line = jnp.stack(p_line)

    number = jnp.arange(entries, dtype=jnp.int32)
    ranks = jnp.arange(limit, dtype=jnp.int32)
    turn = jnp.arange(nz, dtype=jnp.int32)
    earlier = (number[:, None] < number[None, :]).astype(bf16)

    coded = (line_ids % rows + 1) * (2 * rows) + (number % rows + 1)[None, :]
    owners = ((me_z + turn) % nz * ny + me_y)[:, None, None]
    mine = line_ids[None] // rows == owners
    count = dot(mine.astype(bf16).reshape(-1, entries), earlier, 1, 0).astype(jnp.int32)
    rank = jnp.where(mine, count.reshape(mine.shape), -1)
    hit = rank[:, :, None, :] == ranks[:, None]
    table = jnp.sum(jnp.where(hit, coded[None, :, None, :], 0), axis=-1)
    asked_row = table // (2 * rows) - 1
    asked_by = table % (2 * rows) - 1

    sent_p = pick_rows(asked_row, p_line)
    asked_by, sent_p = lax.optimization_barrier((asked_by, sent_p))
    sent_q = pick_rows(jnp.swapaxes(asked_by, 0, 1), q_line.reshape(ny, rows, width))
    got_p = exchange(sent_p, "dp", lines).reshape(slots, width)
    (p_own, q_own), sent_q = gather_chips(both, sent_q)
    got_q = [sent_q[0]]
    got_q += [shifted(sent_q[t], "dp", lambda i, t=t: along_z(i, t)) for t in range(1, nz)]

    p_own, got_q[1] = lax.optimization_barrier((p_own, got_q[1]))
    q_own, got_q[2], got_q[3] = lax.optimization_barrier((q_own, got_q[2], got_q[3]))
    p_other = shifted(p_own, "blk", sibling)
    q_other = shifted(q_own, "blk", sibling)
    where = blk_order(me_blk)

    owner = own_ids // rows
    before = (owner[:, None] == owner[None, :]) & (number[None, :] < number[:, None])
    rank = jnp.sum(before.astype(jnp.int32), axis=1)
    step = owner % ny * nz + (owner // ny - me_z) % nz
    place = (step * limit + rank).reshape(hmax, rows)
    used = jnp.arange(hmax, dtype=jnp.int32)[:, None] < hard_count[None, :]
    used_place = jnp.where(used, place, -1)
    slot = jnp.arange(slots, dtype=jnp.int32)
    weighs = jnp.any(used_place[:, :, None] == slot[None, None, :], axis=0)
    wanted = jnp.where(used, own_ids.reshape(hmax, rows) % rows, 0)[:, :, None]
    own_asked = jnp.sum(
        jnp.where(used_place[:, :, None] == slot[None, None, :], wanted, 0), axis=(0, 1)
    )

    exp_scores, sums = exp_scores_of(q_half, p_own, p_other)
    sums, q_other = lax.optimization_barrier((sums, q_other))
    exp_back, _ = exp_scores_of(p_half, q_own, q_other)
    total, weights, slot_weights, facts = totals_of(
        q_half, got_p, weighs.astype(jnp.float32), sums, positive, length
    )

    peer = jnp.arange(peers, dtype=jnp.int32)
    step_of = (me_z + peer % nz) % nz * ny + peer // nz
    by_slot = jnp.stack([slot_weights[0], own_asked.astype(jnp.float32)])
    by_slot = by_slot.reshape(2, 1, peers, limit)
    to_owner = peer[:, None] == step_of[None, :]
    by_owner = jnp.sum(jnp.where(to_owner[None, :, :, None], by_slot, 0.0), axis=2)
    facts = exchange(facts, "blk")
    facts, by_owner, exp_scores, total = lax.optimization_barrier(
        (facts, by_owner, exp_scores, total)
    )
    got = exchange(jnp.swapaxes(by_owner, 0, 1), "dp")
    from_z = ((me_z - turn) % nz)[:, None] == turn[None, :]
    got = got.reshape(1, nz, ny, 2, limit)
    got = jnp.sum(jnp.where(from_z[:, :, None, None, None], got, 0.0), axis=1)
    got_weights = got[:, :, 0].reshape(1, slots)
    asked = got[:, :, 1].reshape(1, slots).astype(jnp.int32)
    names = asked == jnp.arange(rows, dtype=jnp.int32)[:, None]
    hard_back = jnp.where(names, got_weights, 0.0).astype(bf16)
    facts = facts[where]
    all_total = facts[:, 0].reshape(1, length * rows)
    all_positive = facts[:, 1].reshape(1, length * rows).astype(jnp.int32)

    row = jnp.arange(rows, dtype=jnp.int32)
    column = (where[:, None] * rows + row[None, :]).reshape(1, length * rows)
    own_row = me_blk * rows + row[:, None]
    query_grads = grads_of(
        exp_scores, total, positive[:, None], column,
        p_own, p_other, weights, [got_p], queries, q_scale,
    )
    passage_grads = grads_of(
        exp_back, all_total, own_row, all_positive,
        q_own, q_other, hard_back, got_q, passages, p_scale,
    )
    return (query_grads, passage_grads)


def solution(mesh):
    return jax.shard_map(
        local,
        mesh=mesh,
        in_specs=(
            P(("blk", "dp"), None),
            P(("blk", "dp"), None),
            P(("blk", "dp")),
            P(("blk", "dp"), None),
            P(("blk", "dp")),
        ),
        out_specs=(P(("blk", "dp"), None), P(("blk", "dp"), None)),
        check_vma=False,
    )
```

```python
import jax
import jax.numpy as jnp
from jax import lax
from jax.experimental import pallas as pl
from jax.experimental.pallas import tpu as pltpu
from jax.sharding import PartitionSpec as P

EPS = 1e-06
TAU = 0.02
ROOMY = pltpu.CompilerParams(vmem_limit_bytes=56 * 1024 * 1024)


def unit_rows(x):
    xf = x.astype(jnp.float32)
    scale = lax.rsqrt(jnp.sum(xf * xf, axis=1, keepdims=True) + EPS)
    return (xf * scale, scale)


def unit_kernel(q_ref, p_ref, q_half, p_half, both, q_scale, p_scale):
    for at, x_ref, half, scale in ((0, p_ref, p_half, p_scale), (1, q_ref, q_half, q_scale)):
        unit, factor = unit_rows(x_ref[...])
        half[...] = unit.astype(jnp.bfloat16)
        both[at] = unit.astype(jnp.bfloat16)
        scale[...] = factor


def unit_halves(queries, passages):
    rows, width = queries.shape
    half = jax.ShapeDtypeStruct((rows, width), jnp.bfloat16)
    scale = jax.ShapeDtypeStruct((rows, 1), jnp.float32)
    return pl.pallas_call(
        unit_kernel,
        out_shape=(half, half, jax.ShapeDtypeStruct((2, rows, width), jnp.bfloat16), scale, scale),
        cost_estimate=pl.CostEstimate(
            flops=8 * rows * width, bytes_accessed=12 * rows * width, transcendentals=0
        ),
        name="unit_halves",
    )(queries, passages)


def pick_kernel(index_ref, pool_ref, *out_refs):
    rows = pool_ref.shape[1]
    index = index_ref[0]
    pick = index == lax.broadcasted_iota(jnp.int32, (rows, index.shape[1]), 0)
    found = lax.dot_general(
        pick.astype(jnp.bfloat16),
        pool_ref[0],
        (((0,), (0,)), ((), ())),
        preferred_element_type=jnp.float32,
    )
    found = found.astype(jnp.bfloat16)
    at = 0
    for out_ref in out_refs:
        part = index.shape[1] // len(out_refs)
        out_ref[...] = found[at : at + part].reshape(out_ref.shape)
        at += part


def pick_rows(index, pool, apart=False):
    groups, rows, width = pool.shape
    _, parts, ranks = index.shape
    split = parts if apart else 1
    block = (parts // split, 1, ranks, width)
    whole = (parts // split, groups, ranks, width)
    found = pl.pallas_call(
        pick_kernel,
        grid=(groups,),
        in_specs=[
            pl.BlockSpec((1, 1, parts * ranks), lambda g: (g, 0, 0)),
            pl.BlockSpec((1, rows, width), lambda g: (g, 0, 0)),
        ],
        out_specs=[pl.BlockSpec(block, lambda g: (0, g, 0, 0))] * split,
        out_shape=[jax.ShapeDtypeStruct(whole, jnp.bfloat16)] * split,
        compiler_params=pltpu.CompilerParams(vmem_limit_bytes=4 * 1024 * 1024),
        cost_estimate=pl.CostEstimate(
            flops=2 * groups * rows * parts * ranks * width,
            bytes_accessed=2 * groups * (rows + parts * ranks) * width,
            transcendentals=0,
        ),
        name="pick_rows",
    )(index.reshape(groups, 1, parts * ranks), pool)
    if apart:
        return [part.reshape(groups * ranks, width) for part in found]
    return found[0].reshape(parts, groups * ranks, width)


TILE = 256


def cost(rows, width, columns, exps=0):
    return pl.CostEstimate(
        flops=2 * rows * width * columns,
        bytes_accessed=2 * (rows + columns) * width + 4 * rows * columns,
        transcendentals=exps,
    )


def exp_kernel(x_ref, own_ref, other_ref, exp_ref, sum_ref):
    half = own_ref.shape[0]
    x = x_ref[...]
    added = jnp.zeros(sum_ref.shape, jnp.float32)
    for at, rows_ref in ((0, own_ref), (half, other_ref)):
        for tile in range(0, half, TILE):
            exps = jnp.exp(dot(x, rows_ref[tile : tile + TILE], 1, 1) / TAU)
            exp_ref[:, at + tile : at + tile + TILE] = exps
            added += jnp.sum(exps, axis=1, keepdims=True)
    sum_ref[...] = added


def exp_scores_of(x, own, other):
    rows = x.shape[0]
    return pl.pallas_call(
        exp_kernel,
        out_shape=(
            jax.ShapeDtypeStruct((rows, 2 * own.shape[0]), jnp.float32),
            jax.ShapeDtypeStruct((rows, 1), jnp.float32),
        ),
        compiler_params=ROOMY,
        cost_estimate=cost(rows, x.shape[1], 2 * own.shape[0], 2 * rows * own.shape[0]),
        name="exp_scores",
    )(x, own, other)


def total_kernel(q_ref, hard_ref, mask_ref, sum_ref, positive_ref, total_ref, w_ref, s_ref, facts_ref):
    rows = q_ref.shape[0]
    q = q_ref[...]
    exps = []
    total = sum_ref[...]
    for tile in range(0, hard_ref.shape[0], TILE):
        scores = dot(q, hard_ref[tile : tile + TILE], 1, 1) / TAU
        exps.append(jnp.where(mask_ref[:, tile : tile + TILE] > 0, jnp.exp(scores), 0.0))
        total += jnp.sum(exps[-1], axis=1, keepdims=True)
    total_ref[...] = total
    for number, exp_hard in enumerate(exps):
        tile = number * TILE
        weights = (exp_hard / total).astype(jnp.bfloat16)
        w_ref[:, tile : tile + TILE] = weights
        s_ref[:, tile : tile + TILE] = jnp.sum(weights.astype(jnp.float32), axis=0, keepdims=True)
    across = lax.broadcasted_iota(jnp.int32, (rows, rows), 0)
    down = lax.broadcasted_iota(jnp.int32, (rows, rows), 1)
    total_row = jnp.sum(jnp.where(across == down, total, 0.0), axis=0, keepdims=True)
    for device in range(facts_ref.shape[0]):
        facts_ref[device, 0:1] = total_row
        facts_ref[device, 1:2] = positive_ref[...].astype(jnp.float32)


def totals_of(q_half, hard_rows, mask, sums, positive, length):
    rows = q_half.shape[0]
    slots = hard_rows.shape[0]
    return pl.pallas_call(
        total_kernel,
        out_shape=(
            jax.ShapeDtypeStruct((rows, 1), jnp.float32),
            jax.ShapeDtypeStruct((rows, slots), jnp.bfloat16),
            jax.ShapeDtypeStruct((1, slots), jnp.float32),
            jax.ShapeDtypeStruct((length, 2, rows), jnp.float32),
        ),
        compiler_params=ROOMY,
        cost_estimate=cost(rows, q_half.shape[1], slots, rows * slots),
        name="totals",
    )(q_half, hard_rows, mask, sums, positive.reshape(1, rows))


def grad_kernel(exp_ref, total_ref, mark_ref, marks_ref, own, other, w_ref, x_ref, scale_ref, *rest):
    *chunks, out_ref, hard, sems = rest
    copies = []
    at = 0
    for number, chunk in enumerate(chunks):
        place = hard.at[pl.ds(at, chunk.shape[0])]
        copies.append(pltpu.make_async_copy(chunk, place, sems.at[number]))
        copies[-1].start()
        at += chunk.shape[0]
    half = own.shape[0]
    width = x_ref.shape[1]
    target = (mark_ref[...] == marks_ref[...]).astype(jnp.float32)
    grads = (exp_ref[...] / total_ref[...] - target).astype(jnp.bfloat16)
    weights = w_ref[...]
    scale = scale_ref[...]
    directions = []
    for tile in range(0, width, TILE):
        cols = slice(tile, tile + TILE)
        direction = dot(grads[:, :half], own[:, cols], 1, 0)
        directions.append(direction + dot(grads[:, half:], other[:, cols], 1, 0))
    for copy in copies:
        copy.wait()
    along = jnp.zeros(scale.shape, jnp.float32)
    for number in range(len(directions)):
        cols = slice(number * TILE, (number + 1) * TILE)
        direction = (directions[number] + dot(weights, hard[:, cols], 1, 0)) / TAU
        unit = x_ref[:, cols].astype(jnp.float32) * scale
        along += jnp.sum(unit * direction, axis=1, keepdims=True)
        directions[number] = direction
    for number, direction in enumerate(directions):
        cols = slice(number * TILE, (number + 1) * TILE)
        unit = x_ref[:, cols].astype(jnp.float32) * scale
        out_ref[:, cols] = (scale * (direction - unit * along)).astype(jnp.bfloat16)


def grads_of(exps, total, mark, marks, own, other, weights, hard, x, scale):
    operands = (exps, total, mark, marks, own, other, weights, x, scale)
    whole = pl.BlockSpec(memory_space=pltpu.VMEM)
    return pl.pallas_call(
        grad_kernel,
        in_specs=[whole] * len(operands) + [pl.BlockSpec(memory_space=pl.ANY)] * len(hard),
        out_specs=whole,
        out_shape=jax.ShapeDtypeStruct(x.shape, jnp.bfloat16),
        scratch_shapes=[
            pltpu.VMEM((weights.shape[1], x.shape[1]), jnp.bfloat16),
            pltpu.SemaphoreType.DMA((len(hard),)),
        ],
        compiler_params=ROOMY,
        cost_estimate=cost(*x.shape, exps.shape[1] + weights.shape[1]),
        name="gradients",
    )(*operands, *hard)


def dot(a, b, ca, cb):
    return lax.dot_general(a, b, (((ca,), (cb,)), ((), ())), preferred_element_type=jnp.float32)


def exchange(value, axis, groups=None):
    return lax.all_to_all(
        value, axis, split_axis=0, concat_axis=0, tiled=True, axis_index_groups=groups
    )


def shifted(value, axis, move):
    devices = lax.axis_size(axis)
    return lax.ppermute(value, axis, [(i, move(i)) for i in range(devices)])


def beside(i, step, length):
    half = length // 2
    return i // half * half + (i % half // 2 + step) % (half // 2) * 2 + i % 2


def sibling(i):
    return i // 2 * 2 + 1 - i % 2


def blk_order(me):
    length = lax.axis_size("blk")
    where = []
    for core in range(2):
        for step in range(length // 4):
            for z in range(2):
                there = beside((me + length // 2 * z) % length, -step, length)
                where.append(there // 2 * 2 + (there + core) % 2)
    return jnp.stack(where)


def gather_chips(both, after):
    length = lax.axis_size("blk")

    def turned(value, step):
        return shifted(value, "blk", lambda i: beside(i, step, length))

    over = shifted(both, "blk", lambda i: (i + length // 2) % length)
    over, *after = lax.optimization_barrier((over, *after))
    pair = jnp.stack([both, over])
    right = turned(pair, 1)
    left = turned(pair, -1)
    far = (turned(right[0], 1), turned(left[1], -1))
    blocks = (both, over, right[0], right[1], far[0], far[1], left[0], left[1])
    return [jnp.concatenate([block[k] for block in blocks]) for k in range(2)], after


def local(queries, passages, positive, hard_ids, hard_count):
    rows, width = queries.shape
    hmax = hard_ids.shape[1]
    length = lax.axis_size("blk")
    peers = lax.axis_size("dp")
    me_blk = lax.axis_index("blk")
    me_dp = lax.axis_index("dp")
    nz = 4
    ny = peers // nz
    me_z = me_dp // ny
    me_y = me_dp % ny
    limit = 2 * rows * hmax // peers
    slots = peers * limit
    entries = rows * hmax
    bf16 = jnp.bfloat16

    own_ids = hard_ids.T.reshape(entries)

    q_half, p_half, both, q_scale, p_scale = unit_halves(queries, passages)

    lines = [[z * ny + y for y in range(ny)] for z in range(nz)]
    line_ids = exchange(jnp.broadcast_to(own_ids[None, :], (ny, entries)), "dp", lines)
    q_line = lax.all_gather(q_half, "dp", axis=0, tiled=True, axis_index_groups=lines)

    def along_z(i, step):
        return (i + step * ny) % peers

    p_line = [p_half]
    p_line += [shifted(p_half, "dp", lambda i, t=t: along_z(i, -t)) for t in range(1, nz)]
    p_line = jnp.stack(p_line)

    number = jnp.arange(entries, dtype=jnp.int32)
    ranks = jnp.arange(limit, dtype=jnp.int32)
    turn = jnp.arange(nz, dtype=jnp.int32)
    earlier = (number[:, None] < number[None, :]).astype(bf16)

    coded = (line_ids % rows + 1) * (2 * rows) + (number % rows + 1)[None, :]
    owners = ((me_z + turn) % nz * ny + me_y)[:, None, None]
    mine = line_ids[None] // rows == owners
    count = dot(mine.astype(bf16).reshape(-1, entries), earlier, 1, 0).astype(jnp.int32)
    rank = jnp.where(mine, count.reshape(mine.shape), -1)
    hit = rank[:, :, None, :] == ranks[:, None]
    table = jnp.sum(jnp.where(hit, coded[None, :, None, :], 0), axis=-1)
    asked_row = table // (2 * rows) - 1
    asked_by = table % (2 * rows) - 1

    sent_p = pick_rows(asked_row, p_line)
    asked_by, sent_p = lax.optimization_barrier((asked_by, sent_p))
    sent_q = pick_rows(jnp.swapaxes(asked_by, 0, 1), q_line.reshape(ny, rows, width), True)
    got_p = exchange(sent_p, "dp", lines).reshape(slots, width)
    (p_own, q_own), sent_q = gather_chips(both, sent_q)
    got_q = [sent_q[0]]
    got_q += [shifted(sent_q[t], "dp", lambda i, t=t: along_z(i, t)) for t in range(1, nz)]

    owner = own_ids // rows
    before = (owner[:, None] == owner[None, :]) & (number[None, :] < number[:, None])
    rank = jnp.sum(before.astype(jnp.int32), axis=1)
    step = owner % ny * nz + (owner // ny - me_z) % nz
    place = (step * limit + rank).reshape(hmax, rows)
    used = jnp.arange(hmax, dtype=jnp.int32)[:, None] < hard_count[None, :]
    used_place = jnp.where(used, place, -1)
    slot = jnp.arange(slots, dtype=jnp.int32)
    weighs = jnp.any(used_place[:, :, None] == slot[None, None, :], axis=0)
    wanted = jnp.where(used, own_ids.reshape(hmax, rows) % rows, 0)[:, :, None]
    own_asked = jnp.sum(
        jnp.where(used_place[:, :, None] == slot[None, None, :], wanted, 0), axis=(0, 1)
    )
    mask = weighs.astype(jnp.float32)

    p_own, got_q[1], mask, own_asked = lax.optimization_barrier(
        (p_own, got_q[1], mask, own_asked)
    )
    q_own, got_q[2], got_q[3] = lax.optimization_barrier((q_own, got_q[2], got_q[3]))
    p_other = shifted(p_own, "blk", sibling)
    q_other = shifted(q_own, "blk", sibling)
    where = blk_order(me_blk)

    exp_scores, sums = exp_scores_of(q_half, p_own, p_other)
    sums, q_other = lax.optimization_barrier((sums, q_other))
    exp_back, _ = exp_scores_of(p_half, q_own, q_other)
    total, weights, slot_weights, facts = totals_of(
        q_half, got_p, mask, sums, positive, length
    )

    peer = jnp.arange(peers, dtype=jnp.int32)
    step_of = (me_z + peer % nz) % nz * ny + peer // nz
    by_slot = jnp.stack([slot_weights[0], own_asked.astype(jnp.float32)])
    by_slot = by_slot.reshape(2, 1, peers, limit)
    to_owner = peer[:, None] == step_of[None, :]
    by_owner = jnp.sum(jnp.where(to_owner[None, :, :, None], by_slot, 0.0), axis=2)
    facts = exchange(facts, "blk")
    facts, by_owner, exp_scores, total = lax.optimization_barrier(
        (facts, by_owner, exp_scores, total)
    )
    got = exchange(jnp.swapaxes(by_owner, 0, 1), "dp")
    from_z = ((me_z - turn) % nz)[:, None] == turn[None, :]
    got = got.reshape(1, nz, ny, 2, limit)
    got = jnp.sum(jnp.where(from_z[:, :, None, None, None], got, 0.0), axis=1)
    got_weights = got[:, :, 0].reshape(1, slots)
    asked = got[:, :, 1].reshape(1, slots).astype(jnp.int32)
    names = asked == jnp.arange(rows, dtype=jnp.int32)[:, None]
    hard_back = jnp.where(names, got_weights, 0.0).astype(bf16)
    facts = facts[where]
    all_total = facts[:, 0].reshape(1, length * rows)
    all_positive = facts[:, 1].reshape(1, length * rows).astype(jnp.int32)

    row = jnp.arange(rows, dtype=jnp.int32)
    column = (where[:, None] * rows + row[None, :]).reshape(1, length * rows)
    own_row = me_blk * rows + row[:, None]
    query_grads = grads_of(
        exp_scores, total, positive[:, None], column,
        p_own, p_other, weights, [got_p], queries, q_scale,
    )
    passage_grads = grads_of(
        exp_back, all_total, own_row, all_positive,
        q_own, q_other, hard_back, got_q, passages, p_scale,
    )
    return (query_grads, passage_grads)


def solution(mesh):
    return jax.shard_map(
        local,
        mesh=mesh,
        in_specs=(
            P(("blk", "dp"), None),
            P(("blk", "dp"), None),
            P(("blk", "dp")),
            P(("blk", "dp"), None),
            P(("blk", "dp")),
        ),
        out_specs=(P(("blk", "dp"), None), P(("blk", "dp"), None)),
        check_vma=False,
    )
```

```python
import jax
import jax.numpy as jnp
from jax import lax
from jax.experimental import pallas as pl
from jax.experimental.pallas import tpu as pltpu
from jax.sharding import PartitionSpec as P

EPS = 1e-06
TAU = 0.02
ROOMY = pltpu.CompilerParams(vmem_limit_bytes=56 * 1024 * 1024)


def unit_rows(x):
    xf = x.astype(jnp.float32)
    scale = lax.rsqrt(jnp.sum(xf * xf, axis=1, keepdims=True) + EPS)
    return (xf * scale, scale)


def unit_kernel(q_ref, p_ref, q_half, p_half, both, q_scale, p_scale):
    for at, x_ref, half, scale in ((0, p_ref, p_half, p_scale), (1, q_ref, q_half, q_scale)):
        unit, factor = unit_rows(x_ref[...])
        half[...] = unit.astype(jnp.bfloat16)
        both[at] = unit.astype(jnp.bfloat16)
        scale[...] = factor


def unit_halves(queries, passages):
    rows, width = queries.shape
    half = jax.ShapeDtypeStruct((rows, width), jnp.bfloat16)
    scale = jax.ShapeDtypeStruct((rows, 1), jnp.float32)
    return pl.pallas_call(
        unit_kernel,
        out_shape=(half, half, jax.ShapeDtypeStruct((2, rows, width), jnp.bfloat16), scale, scale),
        cost_estimate=pl.CostEstimate(
            flops=8 * rows * width, bytes_accessed=12 * rows * width, transcendentals=0
        ),
        name="unit_halves",
    )(queries, passages)


def pick_kernel(index_ref, pool_ref, *out_refs):
    rows = pool_ref.shape[1]
    index = index_ref[0]
    pick = index == lax.broadcasted_iota(jnp.int32, (rows, index.shape[1]), 0)
    found = lax.dot_general(
        pick.astype(jnp.bfloat16),
        pool_ref[0],
        (((0,), (0,)), ((), ())),
        preferred_element_type=jnp.float32,
    )
    found = found.astype(jnp.bfloat16)
    at = 0
    for out_ref in out_refs:
        part = index.shape[1] // len(out_refs)
        out_ref[...] = found[at : at + part].reshape(out_ref.shape)
        at += part


def pick_rows(index, pool, apart=False):
    groups, rows, width = pool.shape
    _, parts, ranks = index.shape
    split = parts if apart else 1
    block = (parts // split, 1, ranks, width)
    whole = (parts // split, groups, ranks, width)
    found = pl.pallas_call(
        pick_kernel,
        grid=(groups,),
        in_specs=[
            pl.BlockSpec((1, 1, parts * ranks), lambda g: (g, 0, 0)),
            pl.BlockSpec((1, rows, width), lambda g: (g, 0, 0)),
        ],
        out_specs=[pl.BlockSpec(block, lambda g: (0, g, 0, 0))] * split,
        out_shape=[jax.ShapeDtypeStruct(whole, jnp.bfloat16)] * split,
        compiler_params=pltpu.CompilerParams(vmem_limit_bytes=4 * 1024 * 1024),
        cost_estimate=pl.CostEstimate(
            flops=2 * groups * rows * parts * ranks * width,
            bytes_accessed=2 * groups * (rows + parts * ranks) * width,
            transcendentals=0,
        ),
        name="pick_rows",
    )(index.reshape(groups, 1, parts * ranks), pool)
    if apart:
        return [part.reshape(groups * ranks, width) for part in found]
    return found[0].reshape(parts, groups * ranks, width)


TILE = 256


def cost(rows, width, columns, exps=0):
    return pl.CostEstimate(
        flops=2 * rows * width * columns,
        bytes_accessed=2 * (rows + columns) * width + 4 * rows * columns,
        transcendentals=exps,
    )


def exp_kernel(x_ref, own_ref, other_ref, exp_ref, sum_ref):
    half = own_ref.shape[0]
    x = x_ref[...]
    added = jnp.zeros(sum_ref.shape, jnp.float32)
    for at, rows_ref in ((0, own_ref), (half, other_ref)):
        for tile in range(0, half, TILE):
            exps = jnp.exp(dot(x, rows_ref[tile : tile + TILE], 1, 1) / TAU)
            exp_ref[:, at + tile : at + tile + TILE] = exps
            added += jnp.sum(exps, axis=1, keepdims=True)
    sum_ref[...] = added


def exp_scores_of(x, own, other):
    rows = x.shape[0]
    return pl.pallas_call(
        exp_kernel,
        out_shape=(
            jax.ShapeDtypeStruct((rows, 2 * own.shape[0]), jnp.float32),
            jax.ShapeDtypeStruct((rows, 1), jnp.float32),
        ),
        compiler_params=ROOMY,
        cost_estimate=cost(rows, x.shape[1], 2 * own.shape[0], 2 * rows * own.shape[0]),
        name="exp_scores",
    )(x, own, other)


def total_kernel(q_ref, hard_ref, mask_ref, sum_ref, positive_ref, total_ref, w_ref, s_ref, facts_ref):
    rows = q_ref.shape[0]
    q = q_ref[...]
    exps = []
    total = sum_ref[...]
    for tile in range(0, hard_ref.shape[0], TILE):
        scores = dot(q, hard_ref[tile : tile + TILE], 1, 1) / TAU
        exps.append(jnp.where(mask_ref[:, tile : tile + TILE] > 0, jnp.exp(scores), 0.0))
        total += jnp.sum(exps[-1], axis=1, keepdims=True)
    total_ref[...] = total
    for number, exp_hard in enumerate(exps):
        tile = number * TILE
        weights = (exp_hard / total).astype(jnp.bfloat16)
        w_ref[:, tile : tile + TILE] = weights
        s_ref[:, tile : tile + TILE] = jnp.sum(weights.astype(jnp.float32), axis=0, keepdims=True)
    across = lax.broadcasted_iota(jnp.int32, (rows, rows), 0)
    down = lax.broadcasted_iota(jnp.int32, (rows, rows), 1)
    total_row = jnp.sum(jnp.where(across == down, total, 0.0), axis=0, keepdims=True)
    for device in range(facts_ref.shape[0]):
        facts_ref[device, 0:1] = total_row
        facts_ref[device, 1:2] = positive_ref[...].astype(jnp.float32)


def totals_of(q_half, hard_rows, mask, sums, positive, length):
    rows = q_half.shape[0]
    slots = hard_rows.shape[0]
    return pl.pallas_call(
        total_kernel,
        out_shape=(
            jax.ShapeDtypeStruct((rows, 1), jnp.float32),
            jax.ShapeDtypeStruct((rows, slots), jnp.bfloat16),
            jax.ShapeDtypeStruct((1, slots), jnp.float32),
            jax.ShapeDtypeStruct((length, 2, rows), jnp.float32),
        ),
        compiler_params=ROOMY,
        cost_estimate=cost(rows, q_half.shape[1], slots, rows * slots),
        name="totals",
    )(q_half, hard_rows, mask, sums, positive.reshape(1, rows))


def grad_kernel(exp_ref, total_ref, mark_ref, marks_ref, own, other, w_ref, x_ref, scale_ref, *rest):
    *chunks, out_ref, hard, sems = rest
    copies = []
    at = 0
    for number, chunk in enumerate(chunks):
        place = hard.at[pl.ds(at, chunk.shape[0])]
        copies.append(pltpu.make_async_copy(chunk, place, sems.at[number]))
        copies[-1].start()
        at += chunk.shape[0]
    half = own.shape[0]
    width = x_ref.shape[1]
    target = (mark_ref[...] == marks_ref[...]).astype(jnp.float32)
    grads = (exp_ref[...] / total_ref[...] - target).astype(jnp.bfloat16)
    weights = w_ref[...]
    scale = scale_ref[...]
    directions = []
    for tile in range(0, width, TILE):
        cols = slice(tile, tile + TILE)
        direction = dot(grads[:, :half], own[:, cols], 1, 0)
        directions.append(direction + dot(grads[:, half:], other[:, cols], 1, 0))
    for copy in copies:
        copy.wait()
    along = jnp.zeros(scale.shape, jnp.float32)
    for number in range(len(directions)):
        cols = slice(number * TILE, (number + 1) * TILE)
        direction = (directions[number] + dot(weights, hard[:, cols], 1, 0)) / TAU
        unit = x_ref[:, cols].astype(jnp.float32) * scale
        along += jnp.sum(unit * direction, axis=1, keepdims=True)
        directions[number] = direction
    for number, direction in enumerate(directions):
        cols = slice(number * TILE, (number + 1) * TILE)
        unit = x_ref[:, cols].astype(jnp.float32) * scale
        out_ref[:, cols] = (scale * (direction - unit * along)).astype(jnp.bfloat16)


def grads_of(exps, total, mark, marks, own, other, weights, hard, x, scale):
    operands = (exps, total, mark, marks, own, other, weights, x, scale)
    whole = pl.BlockSpec(memory_space=pltpu.VMEM)
    return pl.pallas_call(
        grad_kernel,
        in_specs=[whole] * len(operands) + [pl.BlockSpec(memory_space=pl.ANY)] * len(hard),
        out_specs=whole,
        out_shape=jax.ShapeDtypeStruct(x.shape, jnp.bfloat16),
        scratch_shapes=[
            pltpu.VMEM((weights.shape[1], x.shape[1]), jnp.bfloat16),
            pltpu.SemaphoreType.DMA((len(hard),)),
        ],
        compiler_params=ROOMY,
        cost_estimate=cost(*x.shape, exps.shape[1] + weights.shape[1]),
        name="gradients",
    )(*operands, *hard)


def dot(a, b, ca, cb):
    return lax.dot_general(a, b, (((ca,), (cb,)), ((), ())), preferred_element_type=jnp.float32)


def exchange(value, axis, groups=None):
    return lax.all_to_all(
        value, axis, split_axis=0, concat_axis=0, tiled=True, axis_index_groups=groups
    )


def shifted(value, axis, move):
    devices = lax.axis_size(axis)
    return lax.ppermute(value, axis, [(i, move(i)) for i in range(devices)])


def beside(i, step, length):
    half = length // 2
    return i // half * half + (i % half // 2 + step) % (half // 2) * 2 + i % 2


def sibling(i):
    return i // 2 * 2 + 1 - i % 2


def blk_order(me):
    length = lax.axis_size("blk")
    where = []
    for core in range(2):
        for step in range(length // 4):
            for z in range(2):
                there = beside((me + length // 2 * z) % length, -step, length)
                where.append(there // 2 * 2 + (there + core) % 2)
    return jnp.stack(where)


def gather_chips(both, after):
    length = lax.axis_size("blk")

    def turned(value, step):
        return shifted(value, "blk", lambda i: beside(i, step, length))

    over = shifted(both, "blk", lambda i: (i + length // 2) % length)
    over, *after = lax.optimization_barrier((over, *after))
    pair = jnp.stack([both, over])
    right = turned(pair, 1)
    left = turned(pair, -1)
    far = (turned(right[0], 1), turned(left[1], -1))
    blocks = (both, over, right[0], right[1], far[0], far[1], left[0], left[1])
    return [jnp.concatenate([block[k] for block in blocks]) for k in range(2)], after


def local(queries, passages, positive, hard_ids, hard_count):
    rows, width = queries.shape
    hmax = hard_ids.shape[1]
    length = lax.axis_size("blk")
    peers = lax.axis_size("dp")
    me_blk = lax.axis_index("blk")
    me_dp = lax.axis_index("dp")
    nz = 4
    ny = peers // nz
    me_z = me_dp // ny
    me_y = me_dp % ny
    limit = 2 * rows * hmax // peers
    slots = peers * limit
    entries = rows * hmax
    bf16 = jnp.bfloat16

    own_ids = hard_ids.T.reshape(entries)

    q_half, p_half, both, q_scale, p_scale = unit_halves(queries, passages)

    lines = [[z * ny + y for y in range(ny)] for z in range(nz)]
    line_ids = exchange(jnp.broadcast_to(own_ids[None, :], (ny, entries)), "dp", lines)
    q_line = lax.all_gather(q_half, "dp", axis=0, tiled=True, axis_index_groups=lines)

    def along_z(i, step):
        return (i + step * ny) % peers

    p_line = [p_half]
    p_line += [shifted(p_half, "dp", lambda i, t=t: along_z(i, -t)) for t in range(1, nz)]
    p_line = jnp.stack(p_line)

    number = jnp.arange(entries, dtype=jnp.int32)
    ranks = jnp.arange(limit, dtype=jnp.int32)
    turn = jnp.arange(nz, dtype=jnp.int32)
    earlier = (number[:, None] < number[None, :]).astype(bf16)

    coded = (line_ids % rows + 1) * (2 * rows) + (number % rows + 1)[None, :]
    owners = ((me_z + turn) % nz * ny + me_y)[:, None, None]
    mine = line_ids[None] // rows == owners
    count = dot(mine.astype(bf16).reshape(-1, entries), earlier, 1, 0).astype(jnp.int32)
    rank = jnp.where(mine, count.reshape(mine.shape), -1)
    hit = rank[:, :, None, :] == ranks[:, None]
    table = jnp.sum(jnp.where(hit, coded[None, :, None, :], 0), axis=-1)
    asked_row = table // (2 * rows) - 1
    asked_by = table % (2 * rows) - 1

    sent_p = pick_rows(asked_row, p_line)
    asked_by, sent_p = lax.optimization_barrier((asked_by, sent_p))
    sent_q = pick_rows(jnp.swapaxes(asked_by, 0, 1), q_line.reshape(ny, rows, width), True)
    got_p = exchange(sent_p, "dp", lines).reshape(slots, width)
    (p_own, q_own), sent_q = gather_chips(both, sent_q)
    got_q = [sent_q[0]]
    got_q += [shifted(sent_q[t], "dp", lambda i, t=t: along_z(i, t)) for t in range(1, nz)]

    owner = own_ids // rows
    before = (owner[:, None] == owner[None, :]) & (number[None, :] < number[:, None])
    rank = jnp.sum(before.astype(jnp.int32), axis=1)
    step = owner % ny * nz + (owner // ny - me_z) % nz
    place = (step * limit + rank).reshape(hmax, rows)
    used = jnp.arange(hmax, dtype=jnp.int32)[:, None] < hard_count[None, :]
    used_place = jnp.where(used, place, -1)
    slot = jnp.arange(slots, dtype=jnp.int32)
    weighs = jnp.any(used_place[:, :, None] == slot[None, None, :], axis=0)
    wanted = jnp.where(used, own_ids.reshape(hmax, rows) % rows, 0)[:, :, None]
    own_asked = jnp.sum(
        jnp.where(used_place[:, :, None] == slot[None, None, :], wanted, 0), axis=(0, 1)
    )
    mask = weighs.astype(jnp.float32)

    p_own, got_q[1], mask, own_asked = lax.optimization_barrier(
        (p_own, got_q[1], mask, own_asked)
    )
    p_other = shifted(p_own, "blk", sibling)
    where = blk_order(me_blk)

    exp_scores, sums = exp_scores_of(q_half, p_own, p_other)
    q_own, got_q[2], got_q[3], sums = lax.optimization_barrier(
        (q_own, got_q[2], got_q[3], sums)
    )
    q_other = shifted(q_own, "blk", sibling)
    exp_back, _ = exp_scores_of(p_half, q_own, q_other)
    total, weights, slot_weights, facts = totals_of(
        q_half, got_p, mask, sums, positive, length
    )

    peer = jnp.arange(peers, dtype=jnp.int32)
    step_of = (me_z + peer % nz) % nz * ny + peer // nz
    by_slot = jnp.stack([slot_weights[0], own_asked.astype(jnp.float32)])
    by_slot = by_slot.reshape(2, 1, peers, limit)
    to_owner = peer[:, None] == step_of[None, :]
    by_owner = jnp.sum(jnp.where(to_owner[None, :, :, None], by_slot, 0.0), axis=2)
    facts = exchange(facts, "blk")
    facts, by_owner, exp_scores, total = lax.optimization_barrier(
        (facts, by_owner, exp_scores, total)
    )
    got = exchange(jnp.swapaxes(by_owner, 0, 1), "dp")
    from_z = ((me_z - turn) % nz)[:, None] == turn[None, :]
    got = got.reshape(1, nz, ny, 2, limit)
    got = jnp.sum(jnp.where(from_z[:, :, None, None, None], got, 0.0), axis=1)
    got_weights = got[:, :, 0].reshape(1, slots)
    asked = got[:, :, 1].reshape(1, slots).astype(jnp.int32)
    names = asked == jnp.arange(rows, dtype=jnp.int32)[:, None]
    hard_back = jnp.where(names, got_weights, 0.0).astype(bf16)
    facts = facts[where]
    all_total = facts[:, 0].reshape(1, length * rows)
    all_positive = facts[:, 1].reshape(1, length * rows).astype(jnp.int32)

    row = jnp.arange(rows, dtype=jnp.int32)
    column = (where[:, None] * rows + row[None, :]).reshape(1, length * rows)
    own_row = me_blk * rows + row[:, None]
    query_grads = grads_of(
        exp_scores, total, positive[:, None], column,
        p_own, p_other, weights, [got_p], queries, q_scale,
    )
    passage_grads = grads_of(
        exp_back, all_total, own_row, all_positive,
        q_own, q_other, hard_back, got_q, passages, p_scale,
    )
    return (query_grads, passage_grads)


def solution(mesh):
    return jax.shard_map(
        local,
        mesh=mesh,
        in_specs=(
            P(("blk", "dp"), None),
            P(("blk", "dp"), None),
            P(("blk", "dp")),
            P(("blk", "dp"), None),
            P(("blk", "dp")),
        ),
        out_specs=(P(("blk", "dp"), None), P(("blk", "dp"), None)),
        check_vma=False,
    )
```

```python
import jax
import jax.numpy as jnp
from jax import lax
from jax.experimental import pallas as pl
from jax.experimental.pallas import tpu as pltpu
from jax.sharding import PartitionSpec as P

EPS = 1e-06
TAU = 0.02
ROOMY = pltpu.CompilerParams(vmem_limit_bytes=56 * 1024 * 1024)


def unit_rows(x):
    xf = x.astype(jnp.float32)
    scale = lax.rsqrt(jnp.sum(xf * xf, axis=1, keepdims=True) + EPS)
    return (xf * scale, scale)


def unit_kernel(q_ref, p_ref, q_half, p_half, both, q_scale, p_scale):
    for at, x_ref, half, scale in ((0, p_ref, p_half, p_scale), (1, q_ref, q_half, q_scale)):
        unit, factor = unit_rows(x_ref[...])
        half[...] = unit.astype(jnp.bfloat16)
        both[at] = unit.astype(jnp.bfloat16)
        scale[...] = factor


def unit_halves(queries, passages):
    rows, width = queries.shape
    half = jax.ShapeDtypeStruct((rows, width), jnp.bfloat16)
    scale = jax.ShapeDtypeStruct((rows, 1), jnp.float32)
    return pl.pallas_call(
        unit_kernel,
        out_shape=(half, half, jax.ShapeDtypeStruct((2, rows, width), jnp.bfloat16), scale, scale),
        cost_estimate=pl.CostEstimate(
            flops=8 * rows * width, bytes_accessed=12 * rows * width, transcendentals=0
        ),
        name="unit_halves",
    )(queries, passages)


def pick_kernel(index_ref, pool_ref, *out_refs):
    rows = pool_ref.shape[1]
    index = index_ref[0]
    pick = index == lax.broadcasted_iota(jnp.int32, (rows, index.shape[1]), 0)
    found = lax.dot_general(
        pick.astype(jnp.bfloat16),
        pool_ref[0],
        (((0,), (0,)), ((), ())),
        preferred_element_type=jnp.float32,
    )
    found = found.astype(jnp.bfloat16)
    at = 0
    for out_ref in out_refs:
        part = index.shape[1] // len(out_refs)
        out_ref[...] = found[at : at + part].reshape(out_ref.shape)
        at += part


def pick_rows(index, pool, apart=False):
    groups, rows, width = pool.shape
    _, parts, ranks = index.shape
    split = parts if apart else 1
    block = (parts // split, 1, ranks, width)
    whole = (parts // split, groups, ranks, width)
    found = pl.pallas_call(
        pick_kernel,
        grid=(groups,),
        in_specs=[
            pl.BlockSpec((1, 1, parts * ranks), lambda g: (g, 0, 0)),
            pl.BlockSpec((1, rows, width), lambda g: (g, 0, 0)),
        ],
        out_specs=[pl.BlockSpec(block, lambda g: (0, g, 0, 0))] * split,
        out_shape=[jax.ShapeDtypeStruct(whole, jnp.bfloat16)] * split,
        compiler_params=pltpu.CompilerParams(vmem_limit_bytes=4 * 1024 * 1024),
        cost_estimate=pl.CostEstimate(
            flops=2 * groups * rows * parts * ranks * width,
            bytes_accessed=2 * groups * (rows + parts * ranks) * width,
            transcendentals=0,
        ),
        name="pick_rows",
    )(index.reshape(groups, 1, parts * ranks), pool)
    if apart:
        return [part.reshape(groups * ranks, width) for part in found]
    return found[0].reshape(parts, groups * ranks, width)


TILE = 256


def cost(rows, width, columns, exps=0):
    return pl.CostEstimate(
        flops=2 * rows * width * columns,
        bytes_accessed=2 * (rows + columns) * width + 4 * rows * columns,
        transcendentals=exps,
    )


def exp_kernel(x_ref, own_ref, other_ref, exp_ref, sum_ref):
    half = own_ref.shape[0]
    x = x_ref[...]
    added = jnp.zeros(sum_ref.shape, jnp.float32)
    for at, rows_ref in ((0, own_ref), (half, other_ref)):
        for tile in range(0, half, TILE):
            exps = jnp.exp(dot(x, rows_ref[tile : tile + TILE], 1, 1) / TAU)
            exp_ref[:, at + tile : at + tile + TILE] = exps
            added += jnp.sum(exps, axis=1, keepdims=True)
    sum_ref[...] = added


def exp_scores_of(x, own, other):
    rows = x.shape[0]
    return pl.pallas_call(
        exp_kernel,
        out_shape=(
            jax.ShapeDtypeStruct((rows, 2 * own.shape[0]), jnp.float32),
            jax.ShapeDtypeStruct((rows, 1), jnp.float32),
        ),
        compiler_params=ROOMY,
        cost_estimate=cost(rows, x.shape[1], 2 * own.shape[0], 2 * rows * own.shape[0]),
        name="exp_scores",
    )(x, own, other)


def total_kernel(q_ref, hard_ref, mask_ref, sum_ref, positive_ref, total_ref, w_ref, s_ref, facts_ref):
    rows = q_ref.shape[0]
    q = q_ref[...]
    exps = []
    total = sum_ref[...]
    for tile in range(0, hard_ref.shape[0], TILE):
        scores = dot(q, hard_ref[tile : tile + TILE], 1, 1) / TAU
        exps.append(jnp.where(mask_ref[:, tile : tile + TILE] > 0, jnp.exp(scores), 0.0))
        total += jnp.sum(exps[-1], axis=1, keepdims=True)
    total_ref[...] = total
    for number, exp_hard in enumerate(exps):
        tile = number * TILE
        weights = (exp_hard / total).astype(jnp.bfloat16)
        w_ref[:, tile : tile + TILE] = weights
        s_ref[:, tile : tile + TILE] = jnp.sum(weights.astype(jnp.float32), axis=0, keepdims=True)
    across = lax.broadcasted_iota(jnp.int32, (rows, rows), 0)
    down = lax.broadcasted_iota(jnp.int32, (rows, rows), 1)
    total_row = jnp.sum(jnp.where(across == down, total, 0.0), axis=0, keepdims=True)
    for device in range(facts_ref.shape[0]):
        facts_ref[device, 0:1] = total_row
        facts_ref[device, 1:2] = positive_ref[...].astype(jnp.float32)


def totals_of(q_half, hard_rows, mask, sums, positive, length):
    rows = q_half.shape[0]
    slots = hard_rows.shape[0]
    return pl.pallas_call(
        total_kernel,
        out_shape=(
            jax.ShapeDtypeStruct((rows, 1), jnp.float32),
            jax.ShapeDtypeStruct((rows, slots), jnp.bfloat16),
            jax.ShapeDtypeStruct((1, slots), jnp.float32),
            jax.ShapeDtypeStruct((length, 2, rows), jnp.float32),
        ),
        compiler_params=ROOMY,
        cost_estimate=cost(rows, q_half.shape[1], slots, rows * slots),
        name="totals",
    )(q_half, hard_rows, mask, sums, positive.reshape(1, rows))


def grad_kernel(exp_ref, total_ref, mark_ref, marks_ref, own, other, w_ref, x_ref, scale_ref, *rest):
    *chunks, out_ref, hard, sems = rest
    copies = []
    at = 0
    for number, chunk in enumerate(chunks):
        place = hard.at[pl.ds(at, chunk.shape[0])]
        copies.append(pltpu.make_async_copy(chunk, place, sems.at[number]))
        copies[-1].start()
        at += chunk.shape[0]
    half = own.shape[0]
    width = x_ref.shape[1]
    target = (mark_ref[...] == marks_ref[...]).astype(jnp.float32)
    grads = (exp_ref[...] / total_ref[...] - target).astype(jnp.bfloat16)
    weights = w_ref[...]
    scale = scale_ref[...]
    directions = []
    for tile in range(0, width, TILE):
        cols = slice(tile, tile + TILE)
        direction = dot(grads[:, :half], own[:, cols], 1, 0)
        directions.append(direction + dot(grads[:, half:], other[:, cols], 1, 0))
    for copy in copies:
        copy.wait()
    along = jnp.zeros(scale.shape, jnp.float32)
    for number in range(len(directions)):
        cols = slice(number * TILE, (number + 1) * TILE)
        direction = (directions[number] + dot(weights, hard[:, cols], 1, 0)) / TAU
        unit = x_ref[:, cols].astype(jnp.float32) * scale
        along += jnp.sum(unit * direction, axis=1, keepdims=True)
        directions[number] = direction
    for number, direction in enumerate(directions):
        cols = slice(number * TILE, (number + 1) * TILE)
        unit = x_ref[:, cols].astype(jnp.float32) * scale
        out_ref[:, cols] = (scale * (direction - unit * along)).astype(jnp.bfloat16)


def grads_of(exps, total, mark, marks, own, other, weights, hard, x, scale):
    operands = (exps, total, mark, marks, own, other, weights, x, scale)
    whole = pl.BlockSpec(memory_space=pltpu.VMEM)
    return pl.pallas_call(
        grad_kernel,
        in_specs=[whole] * len(operands) + [pl.BlockSpec(memory_space=pl.ANY)] * len(hard),
        out_specs=whole,
        out_shape=jax.ShapeDtypeStruct(x.shape, jnp.bfloat16),
        scratch_shapes=[
            pltpu.VMEM((weights.shape[1], x.shape[1]), jnp.bfloat16),
            pltpu.SemaphoreType.DMA((len(hard),)),
        ],
        compiler_params=ROOMY,
        cost_estimate=cost(*x.shape, exps.shape[1] + weights.shape[1]),
        name="gradients",
    )(*operands, *hard)


def dot(a, b, ca, cb):
    return lax.dot_general(a, b, (((ca,), (cb,)), ((), ())), preferred_element_type=jnp.float32)


def exchange(value, axis, groups=None):
    return lax.all_to_all(
        value, axis, split_axis=0, concat_axis=0, tiled=True, axis_index_groups=groups
    )


def shifted(value, axis, move):
    devices = lax.axis_size(axis)
    return lax.ppermute(value, axis, [(i, move(i)) for i in range(devices)])


def beside(i, step, length):
    half = length // 2
    return i // half * half + (i % half // 2 + step) % (half // 2) * 2 + i % 2


def sibling(i):
    return i // 2 * 2 + 1 - i % 2


def blk_order(me):
    length = lax.axis_size("blk")
    where = []
    for core in range(2):
        for step in range(length // 4):
            for z in range(2):
                there = beside((me + length // 2 * z) % length, -step, length)
                where.append(there // 2 * 2 + (there + core) % 2)
    return jnp.stack(where)


def gather_chips(both, after, send):
    length = lax.axis_size("blk")

    def turned(value, step):
        return shifted(value, "blk", lambda i: beside(i, step, length))

    over = shifted(both, "blk", lambda i: (i + length // 2) % length)
    over, *after = lax.optimization_barrier((over, *after))
    pair = jnp.stack([both, over])
    right = turned(pair, 1)
    left = turned(pair, -1)
    after = send(after)
    right, left, after[1] = lax.optimization_barrier((right, left, after[1]))
    far = (turned(right[0], 1), turned(left[1], -1))
    blocks = (both, over, right[0], right[1], far[0], far[1], left[0], left[1])
    return [jnp.concatenate([block[k] for block in blocks]) for k in range(2)], after


def local(queries, passages, positive, hard_ids, hard_count):
    rows, width = queries.shape
    hmax = hard_ids.shape[1]
    length = lax.axis_size("blk")
    peers = lax.axis_size("dp")
    me_blk = lax.axis_index("blk")
    me_dp = lax.axis_index("dp")
    nz = 4
    ny = peers // nz
    me_z = me_dp // ny
    me_y = me_dp % ny
    limit = 2 * rows * hmax // peers
    slots = peers * limit
    entries = rows * hmax
    bf16 = jnp.bfloat16

    own_ids = hard_ids.T.reshape(entries)

    q_half, p_half, both, q_scale, p_scale = unit_halves(queries, passages)

    lines = [[z * ny + y for y in range(ny)] for z in range(nz)]
    line_ids = exchange(jnp.broadcast_to(own_ids[None, :], (ny, entries)), "dp", lines)
    q_line = lax.all_gather(q_half, "dp", axis=0, tiled=True, axis_index_groups=lines)

    def along_z(i, step):
        return (i + step * ny) % peers

    p_line = [p_half]
    p_line += [shifted(p_half, "dp", lambda i, t=t: along_z(i, -t)) for t in range(1, nz)]
    p_line = jnp.stack(p_line)

    number = jnp.arange(entries, dtype=jnp.int32)
    ranks = jnp.arange(limit, dtype=jnp.int32)
    turn = jnp.arange(nz, dtype=jnp.int32)
    earlier = (number[:, None] < number[None, :]).astype(bf16)

    coded = (line_ids % rows + 1) * (2 * rows) + (number % rows + 1)[None, :]
    owners = ((me_z + turn) % nz * ny + me_y)[:, None, None]
    mine = line_ids[None] // rows == owners
    count = dot(mine.astype(bf16).reshape(-1, entries), earlier, 1, 0).astype(jnp.int32)
    rank = jnp.where(mine, count.reshape(mine.shape), -1)
    hit = rank[:, :, None, :] == ranks[:, None]
    table = jnp.sum(jnp.where(hit, coded[None, :, None, :], 0), axis=-1)
    asked_row = table // (2 * rows) - 1
    asked_by = table % (2 * rows) - 1

    sent_p = pick_rows(asked_row, p_line)
    asked_by, sent_p = lax.optimization_barrier((asked_by, sent_p))
    sent_q = pick_rows(jnp.swapaxes(asked_by, 0, 1), q_line.reshape(ny, rows, width), True)
    got_p = exchange(sent_p, "dp", lines).reshape(slots, width)

    def send(chunks):
        turned = [shifted(chunks[t], "dp", lambda i, t=t: along_z(i, t)) for t in range(1, nz)]
        return [chunks[0]] + turned

    (p_own, q_own), got_q = gather_chips(both, sent_q, send)

    owner = own_ids // rows
    before = (owner[:, None] == owner[None, :]) & (number[None, :] < number[:, None])
    rank = jnp.sum(before.astype(jnp.int32), axis=1)
    step = owner % ny * nz + (owner // ny - me_z) % nz
    place = (step * limit + rank).reshape(hmax, rows)
    used = jnp.arange(hmax, dtype=jnp.int32)[:, None] < hard_count[None, :]
    used_place = jnp.where(used, place, -1)
    slot = jnp.arange(slots, dtype=jnp.int32)
    weighs = jnp.any(used_place[:, :, None] == slot[None, None, :], axis=0)
    wanted = jnp.where(used, own_ids.reshape(hmax, rows) % rows, 0)[:, :, None]
    own_asked = jnp.sum(
        jnp.where(used_place[:, :, None] == slot[None, None, :], wanted, 0), axis=(0, 1)
    )
    mask = weighs.astype(jnp.float32)

    p_own, got_q[1], mask, own_asked = lax.optimization_barrier(
        (p_own, got_q[1], mask, own_asked)
    )
    q_own, got_q[2], got_q[3] = lax.optimization_barrier((q_own, got_q[2], got_q[3]))
    p_other = shifted(p_own, "blk", sibling)
    q_other = shifted(q_own, "blk", sibling)
    where = blk_order(me_blk)

    exp_scores, sums = exp_scores_of(q_half, p_own, p_other)
    sums, q_other = lax.optimization_barrier((sums, q_other))
    exp_back, _ = exp_scores_of(p_half, q_own, q_other)
    total, weights, slot_weights, facts = totals_of(
        q_half, got_p, mask, sums, positive, length
    )

    peer = jnp.arange(peers, dtype=jnp.int32)
    step_of = (me_z + peer % nz) % nz * ny + peer // nz
    by_slot = jnp.stack([slot_weights[0], own_asked.astype(jnp.float32)])
    by_slot = by_slot.reshape(2, 1, peers, limit)
    to_owner = peer[:, None] == step_of[None, :]
    by_owner = jnp.sum(jnp.where(to_owner[None, :, :, None], by_slot, 0.0), axis=2)
    facts = exchange(facts, "blk")
    facts, by_owner, exp_scores, total = lax.optimization_barrier(
        (facts, by_owner, exp_scores, total)
    )
    got = exchange(jnp.swapaxes(by_owner, 0, 1), "dp")
    from_z = ((me_z - turn) % nz)[:, None] == turn[None, :]
    got = got.reshape(1, nz, ny, 2, limit)
    got = jnp.sum(jnp.where(from_z[:, :, None, None, None], got, 0.0), axis=1)
    got_weights = got[:, :, 0].reshape(1, slots)
    asked = got[:, :, 1].reshape(1, slots).astype(jnp.int32)
    names = asked == jnp.arange(rows, dtype=jnp.int32)[:, None]
    hard_back = jnp.where(names, got_weights, 0.0).astype(bf16)
    facts = facts[where]
    all_total = facts[:, 0].reshape(1, length * rows)
    all_positive = facts[:, 1].reshape(1, length * rows).astype(jnp.int32)

    row = jnp.arange(rows, dtype=jnp.int32)
    column = (where[:, None] * rows + row[None, :]).reshape(1, length * rows)
    own_row = me_blk * rows + row[:, None]
    query_grads = grads_of(
        exp_scores, total, positive[:, None], column,
        p_own, p_other, weights, [got_p], queries, q_scale,
    )
    passage_grads = grads_of(
        exp_back, all_total, own_row, all_positive,
        q_own, q_other, hard_back, got_q, passages, p_scale,
    )
    return (query_grads, passage_grads)


def solution(mesh):
    return jax.shard_map(
        local,
        mesh=mesh,
        in_specs=(
            P(("blk", "dp"), None),
            P(("blk", "dp"), None),
            P(("blk", "dp")),
            P(("blk", "dp"), None),
            P(("blk", "dp")),
        ),
        out_specs=(P(("blk", "dp"), None), P(("blk", "dp"), None)),
        check_vma=False,
    )
```
